256 devices in a mesh: tm: 32 (over z_hi, x, core), space: 8 (over z_lo, y).
Axes of the slice: x: 4, y: 4, z: 8 (z_hi: 4, z_lo: 2; z = z_hi * 2 + z_lo), core: 2. Of those that a mesh axis runs over, the one named last changes fastest.
Arguments:
- input_frames: bfloat16 [256, 256, 768], P('tm', 'space'), may hold values from -6 to 6
- d_out: bfloat16 [256, 256, 768], P('tm', 'space'), may hold values from -6 to 6
- w_qkv: bfloat16 [768, 2304], replicated, may hold values from -0.21875 to 0.21875
- w_out: bfloat16 [768, 768], replicated, may hold values from -0.21875 to 0.21875
Outputs:
- input_gradient: bfloat16 [256, 256, 768], P('tm', 'space')
- grad_qkv: float32 [768, 2304], P(('tm', 'space'))
- grad_out: float32 [768, 768], P(('tm', 'space'))
The draws below stay inside these ranges and needn't reach their ends.
All inputs are finite; a program needn't handle non-finite values.
Results may differ from the reference program's by a relative error of at most 0.013.
Values may be sent and summed in bfloat16 or wider, within the bound.
No kernel may reach another device: no remote copies, remote signals or barrier semaphores. Data moves between devices by JAX's collectives and lax.ppermute only.
A program may use at most 128 MiB of HBM per device.

```python
import jax
import jax.numpy as jnp
from jax import lax

D = 768
HEADS = 12
FRAMES = 256
PATCHES = 256


def levels(rng, dims, split, smallest, high):
    factor_of = 1.0
    for position, blocks in split:
        heights = jax.random.uniform(jax.random.fold_in(jax.random.fold_in(rng, 6), position), (blocks,), jnp.float32, smallest / len(split), high / len(split))
        factor_of = factor_of * jnp.repeat(jnp.exp(heights), dims[position] // blocks).reshape((-1,) + (1,) * (len(dims) - 1 - position))
    return factor_of


def gaussian(key, shape, scale, limit, shards=(), kind=jnp.bfloat16):
    values = scale * jax.random.normal(key, shape, jnp.float32)
    if shards:
        values = values * levels(key, shape, shards, -0.22, 0.18)
    return jnp.clip(values, -limit, limit).astype(kind)


def setup_inputs(seed: int = 0) -> dict:
    arg_keys = jax.random.split(jax.random.key(seed), 5)
    return {
        "input_frames": gaussian(arg_keys[0], (FRAMES, PATCHES, D), 1.0, 6.0, ((0, 32), (1, 8))),
        "d_out": gaussian(arg_keys[1], (FRAMES, PATCHES, D), 1.0, 6.0, ((0, 32), (1, 8))),
        "w_qkv": gaussian(arg_keys[2], (D, 3 * D), D ** -0.5, 0.21875),
        "w_out": gaussian(arg_keys[3], (D, D), D ** -0.5, 0.21875),
    }


def patch_backward(pair):
    qkv_p, dattn_p = pair
    frames = qkv_p.shape[0]
    feature_width = dattn_p.shape[1]
    head_dim = feature_width // HEADS
    scale = 1.0 / head_dim ** 0.5
    parts = qkv_p.astype(jnp.float32).reshape(frames, 3, HEADS, head_dim)
    query, keys, values = (parts[:, 0], parts[:, 1], parts[:, 2])
    scores = jnp.einsum('fhe,ghe->hfg', query, keys) * scale
    probs = jax.nn.softmax(scores, axis=-1)
    probs_b = lax.optimization_barrier(probs.astype(jnp.bfloat16)).astype(jnp.float32)
    attn = jnp.einsum('hfg,ghe->fhe', probs_b, values).astype(jnp.bfloat16)
    dattn = dattn_p.astype(jnp.float32).reshape(frames, HEADS, head_dim)
    dvalue = jnp.einsum('hfg,fhe->ghe', probs_b, dattn).astype(jnp.bfloat16)
    dprobs = jnp.einsum('fhe,ghe->hfg', dattn, values)
    delta = lax.optimization_barrier(jnp.sum(dattn * attn.astype(jnp.float32), axis=-1))
    dscores = probs * (dprobs - jnp.transpose(delta)[:, :, None]) * scale
    dscores_b = lax.optimization_barrier(dscores.astype(jnp.bfloat16)).astype(jnp.float32)
    dquery = jnp.einsum('hfg,ghe->fhe', dscores_b, keys).astype(jnp.bfloat16)
    dkey = jnp.einsum('hfg,fhe->ghe', dscores_b, query).astype(jnp.bfloat16)
    dqkv = jnp.stack([dquery, dkey, dvalue], axis=1).reshape(frames, 3 * feature_width)
    return (attn.reshape(frames, feature_width), dqkv)

def reference(input_frames, d_out, w_qkv, w_out):
    frames, patches, feature_width = input_frames.shape
    token_rows = frames * patches
    x_rows = input_frames.reshape(token_rows, feature_width).astype(jnp.float32)
    row_mean = lax.optimization_barrier(jnp.mean(x_rows, axis=1, keepdims=True))
    centered_rows = x_rows - row_mean
    inverse_deviation = 1.0 / jnp.sqrt(lax.optimization_barrier(jnp.mean(centered_rows * centered_rows, axis=1, keepdims=True)) + 1e-05)
    standardized_input = centered_rows * inverse_deviation
    normalized_rows = standardized_input.astype(jnp.bfloat16)
    qkv = jnp.dot(normalized_rows, w_qkv, preferred_element_type=jnp.float32).astype(jnp.bfloat16)
    output_gradient_rows = d_out.reshape(token_rows, feature_width)
    dattn = jnp.dot(output_gradient_rows, jnp.transpose(w_out), preferred_element_type=jnp.float32).astype(jnp.bfloat16)
    qkv_t = jnp.transpose(qkv.reshape(frames, patches, 3 * feature_width), (1, 0, 2))
    dattn_t = jnp.transpose(dattn.reshape(frames, patches, feature_width), (1, 0, 2))
    attn_t, dqkv_t = lax.map(patch_backward, (qkv_t, dattn_t))
    attn = jnp.transpose(attn_t, (1, 0, 2)).reshape(token_rows, feature_width)
    dqkv = jnp.transpose(dqkv_t, (1, 0, 2)).reshape(token_rows, 3 * feature_width)
    grad_out = jnp.dot(jnp.transpose(attn), output_gradient_rows, preferred_element_type=jnp.float32)
    grad_qkv = jnp.dot(jnp.transpose(normalized_rows), dqkv, preferred_element_type=jnp.float32)
    normalized_gradient = jnp.dot(dqkv, jnp.transpose(w_qkv), preferred_element_type=jnp.float32)
    first_term = lax.optimization_barrier(jnp.mean(normalized_gradient, axis=1, keepdims=True))
    second_term = lax.optimization_barrier(jnp.mean(normalized_gradient * standardized_input, axis=1, keepdims=True))
    input_gradient = output_gradient_rows.astype(jnp.float32) + inverse_deviation * (normalized_gradient - first_term - standardized_input * second_term)
    return (input_gradient.astype(jnp.bfloat16).reshape(frames, patches, feature_width), grad_qkv, grad_out)
```

```python
import functools

import jax
import jax.numpy as jnp
import numpy as np
from jax import lax
from jax.experimental import pallas as pl
from jax.experimental.pallas import tpu as pltpu
from jax.sharding import Mesh, PartitionSpec as P

HEAD = 64
BF = jnp.bfloat16
F32 = jnp.float32
VM = pl.BlockSpec(memory_space=pltpu.VMEM)
SM = pl.BlockSpec(memory_space=pltpu.SMEM)


def nn(a, b):
    return lax.dot_general(a, b, (((1,), (0,)), ((), ())), preferred_element_type=F32)


def nt(a, b):
    return lax.dot_general(a, b, (((1,), (1,)), ((), ())), preferred_element_type=F32)


def call(body, outs, ins, scratch=(), smem=(), flops=0, nbytes=0, limit=48):
    return pl.pallas_call(
        body,
        out_shape=[jax.ShapeDtypeStruct(s, d) for s, d in outs],
        in_specs=[SM if i in smem else VM for i in range(len(ins))],
        out_specs=[VM] * len(outs),
        scratch_shapes=list(scratch),
        compiler_params=pltpu.CompilerParams(vmem_limit_bytes=limit * 2**20),
        cost_estimate=pl.CostEstimate(flops=flops, bytes_accessed=nbytes, transcendentals=0),
    )(*ins)


def selection(rows, source):
    at = lax.broadcasted_iota(jnp.int32, (rows, source.shape[1]), 0)
    return (at == source).astype(F32).astype(BF)


def home_table():
    f, p = np.divmod(np.arange(256), 32)
    return ((p // 2) * 16 + (p % 2) * 8 + f).astype(np.int32)[None]


def feature_table(n):
    f = np.arange(n)
    d, j = f // 3, f % 3
    s8, up = d % 8, d // 8
    return (s8 * (n // 8) + up * 3 + j).astype(np.int32)[None]


def second_table():
    out = np.full((8, 384), -4096, np.int32)
    out[2] = 0
    for i in range(384):
        if i < 288:
            t, rem = divmod(i, 96)
            half = 0
        else:
            t, rem = 3, (i - 288) % 48
            half = (i - 288) // 48
        zh, rem = divmod(rem, 24)
        x, rem = divmod(rem, 6)
        c, j = divmod(rem, 3)
        if t < 2:
            row, half = j, t
        elif t == 2:
            row, half = 3 + j // 2, j % 2
        else:
            row = 5 + j
            out[2, i] = 32
        out[half, i] = (x * 4 + zh) * 16 + c * 8 + row
    return out


def pack_body(x_ref, d_ref, home_ref, o_ref):
    sel = selection(256, home_ref[...])
    o_ref[:, 0:16, :] = nn(sel, x_ref[...]).astype(BF).reshape(16, 16, 768)
    o_ref[:, 16:32, :] = nn(sel, d_ref[...]).astype(BF).reshape(16, 16, 768)


def rows_of(ref, first):
    start = first // 16 * 16
    block = ref[:, start : start + 16, :].astype(F32)
    return block[:, first - start : first - start + 8, :].reshape(128, 768)


def normalize(x):
    mean = jnp.mean(x, axis=1, keepdims=True)
    cen = x - mean
    inv = 1.0 / jnp.sqrt(jnp.mean(cen * cen, axis=1, keepdims=True) + 1e-05)
    return cen * inv, inv


def main_body(own_ref, oth_ref, w_ref, wo_ref, feat_ref, feat2_ref, g_ref, dqkv_ref,
              n_s, d_s, qkv_s, a_s, kt_s, vt_s, at_s, dqt_s, att_s, nt_s):
    for patch in range(2):
        for side, ref in enumerate((own_ref, oth_ref)):
            at = patch * 256 + side * 128
            n_s[at : at + 128, :] = normalize(rows_of(ref, patch * 8))[0].astype(BF)
            d_s[at : at + 128, :] = rows_of(ref, 16 + patch * 8).astype(BF)
    for t in range(3):
        qkv_s[:, t * 384 : (t + 1) * 384] = nn(n_s[...], w_ref[:, t * 384 : (t + 1) * 384]).astype(BF)
    a_s[...] = nt(d_s[...], wo_ref[...]).astype(BF)
    kt_s[...] = (qkv_s[:, 384:768] * 0.125).T
    vt_s[...] = qkv_s[:, 768:1152].T
    at_s[...] = a_s[...].T
    lane = lax.broadcasted_iota(jnp.int32, (1, 128), 1)

    def unit(u, carry):
        patch, pair = u // 3, lax.rem(u, 3)
        rows = pl.ds(pl.multiple_of(patch * 256, 256), 256)

        def cols(base):
            return pl.ds(pl.multiple_of(base + pair * 128, 128), 128)

        q = qkv_s[rows, cols(0)] * 0.125
        k = qkv_s[rows, cols(384)]
        v = qkv_s[rows, cols(768)]
        a = a_s[rows, cols(0)]
        dks, dvs = [], []
        for h in range(2):
            keep = ((lane >= h * HEAD) & (lane < (h + 1) * HEAD)).astype(F32).astype(BF)
            hr = pl.ds(pl.multiple_of(pair * 128 + h * HEAD, HEAD), HEAD)
            qh, ah = q * keep, a * keep
            st = nt(k, qh)
            e = jnp.exp(st - jnp.max(st, axis=0, keepdims=True))
            p = e * (1.0 / jnp.sum(e, axis=0, keepdims=True))
            pb = p.astype(BF)
            attn = nn(vt_s[hr, rows], pb).astype(BF)
            att_s[hr, rows] = attn
            delta = jnp.sum(at_s[hr, rows].astype(F32) * attn.astype(F32), axis=0, keepdims=True)
            ds = (p * (nt(v, ah) - delta)).astype(BF)
            dqt_s[hr, rows] = nn(kt_s[hr, rows], ds).astype(BF)
            dvs.append(nn(pb, ah))
            dks.append(nn(ds, qh))
        dqkv_ref[rows, cols(384)] = (dks[0] + dks[1]).astype(BF)
        dqkv_ref[rows, cols(768)] = (dvs[0] + dvs[1]).astype(BF)
        return carry

    lax.fori_loop(0, 6, unit, 0)
    dqkv_ref[:, 0:384] = dqt_s[...].T
    nt_s[...] = nt(selection(768, feat_ref[...]), n_s[...]).astype(BF)
    for t in range(3):
        g = nn(nt_s[...], dqkv_ref[:, t * 384 : (t + 1) * 384]).astype(BF)
        g_ref[:, t * 96 : (t + 1) * 96, :] = g.reshape(8, 96, 384)
    attp = nn(selection(384, feat2_ref[...]), att_s[...]).astype(BF)
    for t in range(2):
        g = nn(attp, d_s[:, t * 384 : (t + 1) * 384]).astype(BF)
        g_ref[:, 288 + t * 48 : 288 + (t + 1) * 48, :] = g.reshape(8, 48, 384)


def dnormed_body(dqkv_ref, w_ref, own_ref, oth_ref):
    part = nt(dqkv_ref[...], w_ref[...])
    for patch in range(2):
        own_ref[patch * 128 : (patch + 1) * 128, :] = part[patch * 256 : patch * 256 + 128]
        oth_ref[patch * 128 : (patch + 1) * 128, :] = part[patch * 256 + 128 : patch * 256 + 256].astype(BF)


def input_gradient_body(part_ref, got_ref, own_ref, o_ref):
    outs = []
    for patch in range(2):
        xhat, inv = normalize(rows_of(own_ref, patch * 8))
        dout = rows_of(own_ref, 16 + patch * 8)
        at = pl.ds(patch * 128, 128)
        dn = part_ref[at, :] + got_ref[at, :].astype(F32)
        first = jnp.mean(dn, axis=1, keepdims=True)
        second = jnp.mean(dn * xhat, axis=1, keepdims=True)
        outs.append((dout + inv * (dn - first - xhat * second)).reshape(16, 8, 768))
    o_ref[...] = jnp.concatenate(outs, axis=1).astype(BF)


def second_body(core_ref, r_ref, ig_ref, table_ref, o_ref):
    total = r_ref[0].astype(F32)
    for s in range(1, 8):
        total = total + r_ref[s].astype(F32)
    total = total.astype(BF)
    shift = table_ref[2:3, :] * core_ref[0]
    o_ref[:, 0:16, :] = ig_ref[...]
    for h in range(2):
        part = nn(selection(256, table_ref[h : h + 1, :] + shift), total).astype(BF)
        o_ref[:, 16:32, h * 384 : (h + 1) * 384] = part.reshape(16, 16, 384)


def home_body(core_ref, r_ref, home_ref, ig_ref, own_ref, oth_ref):
    sel = selection(256, home_ref[...])
    back = lax.dot_general(
        sel, r_ref[:, 0:16, :].reshape(256, 768), (((0,), (0,)), ((), ())), preferred_element_type=F32
    )
    ig_ref[...] = back.astype(BF)
    total = r_ref[0, 16:32, :].astype(F32)
    for s in range(1, 16):
        total = total + r_ref[s, 16:32, :].astype(F32)
    low = core_ref[0] == 0
    own_ref[...] = jnp.where(low, total[0:8], total[8:16])
    oth_ref[...] = jnp.where(low, total[8:16], total[0:8])


def last_body(core_ref, own_ref, got_ref, gq_ref, go_ref):
    own, got = own_ref[...], got_ref[...]
    low = core_ref[0] == 0
    halves = (jnp.where(low, own, got), jnp.where(low, got, own))
    for h, m in enumerate(halves):
        at = h * 384
        gq_ref[:, at : at + 384] = m[0:3, 0:384]
        gq_ref[:, 768 + at : 768 + at + 384] = m[0:3, 384:768]
        gq_ref[0:1, 1536 + at : 1536 + at + 384] = m[3:4, 0:384]
        gq_ref[1:2, 1536 + at : 1536 + at + 384] = m[3:4, 384:768]
        gq_ref[2:3, 1536 + at : 1536 + at + 384] = m[4:5, 0:384]
    go_ref[...] = own[5:8] + got[5:8]


def local(x, d, w_qkv, w_out):
    core = lax.axis_index("c")
    core1 = core.reshape(1).astype(jnp.int32)
    home = jnp.asarray(home_table())
    feat, feat2 = jnp.asarray(feature_table(768)), jnp.asarray(feature_table(384))
    slots = jnp.asarray(second_table())

    def swap(v):
        return lax.ppermute(v, "c", [(0, 1), (1, 0)])

    packed, = call(pack_body, [((16, 32, 768), BF)], [x.reshape(256, 768), d.reshape(256, 768), home])
    own = lax.all_to_all(packed, ("x", "zh"), split_axis=0, concat_axis=0, tiled=True)
    oth = swap(own)
    w = lax.dynamic_slice(w_qkv.reshape(768, 3, 768), (0, 0, core * 384), (768, 3, 384)).reshape(768, 1152)
    wo = lax.dynamic_slice(w_out, (core * 384, 0), (384, 768))
    scr = lambda *s: pltpu.VMEM(s, BF)
    grads, dqkv = call(
        main_body,
        [((8, 384, 384), BF), ((512, 1152), BF)],
        [own, oth, w, wo, feat, feat2],
        scratch=[scr(512, 768), scr(512, 768), scr(512, 1152), scr(512, 384), scr(384, 512), scr(384, 512),
                 scr(384, 512), scr(384, 512), scr(384, 512), scr(768, 512)],
        flops=6 * 10**9,
        nbytes=10**7,
    )
    part = lax.all_to_all(grads, ("zl", "y"), split_axis=0, concat_axis=0, tiled=True)
    mine, theirs = call(
        dnormed_body, [((256, 768), F32), ((256, 768), BF)], [dqkv, w], flops=10**9, nbytes=5 * 10**6
    )
    got = swap(theirs)
    ig, = call(input_gradient_body, [((16, 16, 768), BF)], [mine, got, own], nbytes=3 * 10**6)
    mixed, = call(second_body, [((16, 32, 768), BF)], [core1, part, ig, slots], smem=(0,))
    back = lax.all_to_all(mixed, ("x", "zh"), split_axis=0, concat_axis=0, tiled=True)
    ig_home, own8, oth8 = call(
        home_body, [((256, 768), BF), ((8, 768), F32), ((8, 768), F32)], [core1, back, home], smem=(0,)
    )
    grad_qkv, grad_out = call(
        last_body, [((3, 2304), F32), ((3, 768), F32)], [core1, own8, swap(oth8)], smem=(0,)
    )
    return ig_home.reshape(8, 32, 768), grad_qkv, grad_out


def solution(mesh):
    fine = Mesh(mesh.devices.reshape(4, 4, 2, 2, 4), ("zh", "x", "c", "zl", "y"))
    tm, space = ("zh", "x", "c"), ("zl", "y")
    tokens, rows = P(tm, space, None), P(tm + space, None)
    return jax.shard_map(
        local,
        mesh=fine,
        in_specs=(tokens, tokens, P(), P()),
        out_specs=(tokens, rows, rows),
        check_vma=False,
    )
```

```python
import jax
import jax.numpy as jnp
from jax import lax
from jax.experimental import pallas as pl
from jax.experimental.pallas import tpu as pltpu
from jax.sharding import Mesh, PartitionSpec as P

HEAD = 64
BF = jnp.bfloat16
F32 = jnp.float32
VM = pl.BlockSpec(memory_space=pltpu.VMEM)
SM = pl.BlockSpec(memory_space=pltpu.SMEM)
HB = pl.BlockSpec(memory_space=pltpu.HBM)


def nn(a, b):
    return lax.dot_general(a, b, (((1,), (0,)), ((), ())), preferred_element_type=F32)


def nt(a, b):
    return lax.dot_general(a, b, (((1,), (1,)), ((), ())), preferred_element_type=F32)


def call(body, outs, ins, scratch=(), smem=(), hbm=(), flops=0, nbytes=0, limit=16):
    space = {i: SM for i in smem} | {i: HB for i in hbm}
    return pl.pallas_call(
        body,
        out_shape=[jax.ShapeDtypeStruct(s, d) for s, d in outs],
        in_specs=[space.get(i, VM) for i in range(len(ins))],
        out_specs=[VM] * len(outs),
        scratch_shapes=list(scratch),
        compiler_params=pltpu.CompilerParams(vmem_limit_bytes=limit * 2**20),
        cost_estimate=pl.CostEstimate(flops=flops, bytes_accessed=nbytes, transcendentals=0),
    )(*ins)


def selection(rows, source):
    at = lax.broadcasted_iota(jnp.int32, (rows, source.shape[1]), 0)
    return (at == source).astype(F32).astype(BF)


def lanes(n):
    return lax.broadcasted_iota(jnp.int32, (1, n), 1)


def third(i):
    return (i * 21846) >> 16


def home_order():
    i = lanes(256)
    f, p = i >> 5, i & 31
    return ((p >> 1) << 4) + ((p & 1) << 3) + f


def feature_order(n, x0, y0):
    f = lanes(n)
    d = third(f)
    c = (d >> 3) & 1
    x, y = (((d >> 4) & 3) - x0) & 3, ((d & 3) - y0) & 3
    first, second = jnp.where(c == 0, x, y), jnp.where(c == 0, y, x)
    low = (d >> 6) * 6 + ((d >> 2) & 1) * 3 + (f - 3 * d)
    return c * (n // 2) + first * (n // 8) + second * (n // 32) + low


def split_order():
    i = lanes(384)
    m = jnp.where(i < 96, 0, jnp.where(i < 192, 1, 2))
    hh = jnp.where(i < 336, 0, 1)
    low, high = i - 96 * m, i - 288 - 48 * hh
    t1 = jnp.where(low < 24, 0, jnp.where(low < 48, 1, jnp.where(low < 72, 2, 3)))
    t2 = jnp.where(high < 12, 0, jnp.where(high < 24, 1, jnp.where(high < 36, 2, 3)))
    return jnp.where(i < 288, t1 * 72 + m * 24 + low, t2 * 84 + 72 + hh * 12 + high)


def slot_order(core):
    i = lanes(192)
    c = jnp.where(i < 96, 0, 1)
    i = i - 96 * c
    big = i < 72
    m = jnp.where(i < 24, 0, jnp.where(i < 48, 1, 2))
    hh = jnp.where(i < 84, 0, 1)
    rem = jnp.where(big, i - 24 * m, i - 72 - 12 * hh)
    d = third(rem)
    j = rem - 3 * d
    row = jnp.where(big, jnp.where(m < 2, j, 3 + (j >> 1)), 5 + j)
    half = jnp.where(big, jnp.where(m < 2, m, j & 1), hh)
    return ((d + jnp.where(big, 0, 4 * core)) << 4) + (c << 3) + row, half


def pack_body(x_ref, d_ref, o_ref, x_s, d_s, sems):
    copies = [pltpu.make_async_copy(r, s, sems.at[i]) for i, (r, s) in enumerate(((x_ref, x_s), (d_ref, d_s)))]
    for copy in copies:
        copy.start()
    sel = selection(256, home_order())
    copies[0].wait()
    o_ref[:, 0:16, :] = nn(sel, x_s[...]).astype(BF).reshape(16, 16, 768)
    copies[1].wait()
    o_ref[:, 16:32, :] = nn(sel, d_s[...]).astype(BF).reshape(16, 16, 768)


def rows_of(ref, first):
    start = first // 16 * 16
    block = ref[:, start : start + 16, :].astype(F32)
    return block[:, first - start : first - start + 8, :].reshape(128, 768)


def normalize(x):
    mean = jnp.mean(x, axis=1, keepdims=True)
    cen = x - mean
    inv = 1.0 / jnp.sqrt(jnp.mean(cen * cen, axis=1, keepdims=True) + 1e-05)
    return cen * inv, inv


def weight_copies(core, source, target, sems):
    copies = []
    for t in range(3):
        cols = pl.ds(pl.multiple_of(t * 768 + core * 384, 128), 384)
        copies.append(pltpu.make_async_copy(source.at[:, cols], target.at[:, t * 384 : (t + 1) * 384], sems.at[t]))
    return copies


def main_body(at_ref, own_ref, oth_ref, wqkv_ref, wout_ref, dqkv_ref, *rest):
    g_refs = rest[:8]
    (n_s, d_s, qkv_s, a_s, kt_s, vt_s, at_s, dqt_s, att_s, nt_s, w_ref, wo_ref,
     sems) = rest[8:]
    copies = weight_copies(at_ref[0], wqkv_ref, w_ref, sems)
    rows = pl.ds(pl.multiple_of(at_ref[0] * 384, 128), 384)
    copies.append(pltpu.make_async_copy(wout_ref.at[rows, :], wo_ref, sems.at[3]))
    for copy in copies:
        copy.start()
    for patch in range(2):
        for side, ref in enumerate((own_ref, oth_ref)):
            at = patch * 256 + side * 128
            n_s[at : at + 128, :] = normalize(rows_of(ref, patch * 8))[0].astype(BF)
            d_s[at : at + 128, :] = rows_of(ref, 16 + patch * 8).astype(BF)
    for t in range(3):
        copies[t].wait()
        qkv_s[:, t * 384 : (t + 1) * 384] = nn(n_s[...], w_ref[:, t * 384 : (t + 1) * 384]).astype(BF)
    copies[3].wait()
    a_s[...] = nt(d_s[...], wo_ref[...]).astype(BF)
    kt_s[...] = (qkv_s[:, 384:768] * 0.125).T
    vt_s[...] = qkv_s[:, 768:1152].T
    at_s[...] = a_s[...].T
    lane = lax.broadcasted_iota(jnp.int32, (1, 128), 1)

    keeps = [((lane >= h * HEAD) & (lane < (h + 1) * HEAD)).astype(F32).astype(BF) for h in range(2)]
    work = []
    for pair in range(3):
        for patch in range(2):
            rows, at = slice(patch * 256, (patch + 1) * 256), pair * 128
            q = qkv_s[rows, at : at + 128] * 0.125
            k = qkv_s[rows, 384 + at : 384 + at + 128]
            v = qkv_s[rows, 768 + at : 768 + at + 128]
            a = a_s[rows, at : at + 128]
            for h in range(2):
                work.append((rows, at, slice(at + h * HEAD, at + (h + 1) * HEAD), q * keeps[h], a * keeps[h], k, v))
    sts = [nt(k, qh) for _, _, _, qh, _, k, _ in work]
    dps = [nt(v, ah) for _, _, _, _, ah, _, v in work]
    ps = []
    for st in sts:
        e = jnp.exp(st - jnp.max(st, axis=0, keepdims=True))
        ps.append(e * (1.0 / jnp.sum(e, axis=0, keepdims=True)))
    pbs = [p.astype(BF) for p in ps]
    dss = []
    for (rows, _, hr, _, _, _, _), p, pb, dp in zip(work, ps, pbs, dps):
        attn = nn(vt_s[hr, rows], pb).astype(BF)
        att_s[hr, rows] = attn
        delta = jnp.sum(at_s[hr, rows].astype(F32) * attn.astype(F32), axis=0, keepdims=True)
        dss.append((p * (dp - delta)).astype(BF))
    for i in range(0, 12, 2):
        rows, at = work[i][:2]
        dv = nn(pbs[i], work[i][4]) + nn(pbs[i + 1], work[i + 1][4])
        dk = nn(dss[i], work[i][3]) + nn(dss[i + 1], work[i + 1][3])
        dqkv_ref[rows, 768 + at : 768 + at + 128] = dv.astype(BF)
        dqkv_ref[rows, 384 + at : 384 + at + 128] = dk.astype(BF)
    for (rows, _, hr, _, _, _, _), ds in zip(work, dss):
        dqt_s[hr, rows] = nn(kt_s[hr, rows], ds).astype(BF)
    dqkv_ref[:, 0:384] = dqt_s[...].T
    nt_s[...] = nt(selection(768, feature_order(768, at_ref[1], at_ref[2])), n_s[...]).astype(BF)
    for t in range(3):
        g = nn(nt_s[...], dqkv_ref[:, t * 384 : (t + 1) * 384]).astype(BF)
        for i, ref in enumerate(g_refs):
            ref[t * 96 : (t + 1) * 96, :] = g[i * 96 : (i + 1) * 96]
    attp = nn(selection(384, feature_order(384, at_ref[1], at_ref[2])), att_s[...]).astype(BF)
    for t in range(2):
        g = nn(attp, d_s[:, t * 384 : (t + 1) * 384]).astype(BF)
        for i, ref in enumerate(g_refs):
            ref[288 + t * 48 : 288 + (t + 1) * 48, :] = g[i * 48 : (i + 1) * 48]


def dnormed_body(at_ref, dqkv_ref, wqkv_ref, mine_ref, theirs_ref, w_ref, sems):
    copies = weight_copies(at_ref[0], wqkv_ref, w_ref, sems)
    for copy in copies:
        copy.start()
    for copy in copies:
        copy.wait()
    part = nt(dqkv_ref[...], w_ref[...])
    for patch in range(2):
        mine_ref[patch * 128 : (patch + 1) * 128, :] = part[patch * 256 : patch * 256 + 128]
        theirs_ref[patch * 128 : (patch + 1) * 128, :] = part[patch * 256 + 128 : patch * 256 + 256].astype(BF)


def input_gradient_body(part_ref, got_ref, own_ref, o_ref):
    outs = []
    for patch in range(2):
        xhat, inv = normalize(rows_of(own_ref, patch * 8))
        dout = rows_of(own_ref, 16 + patch * 8)
        at = pl.ds(patch * 128, 128)
        dn = part_ref[at, :] + got_ref[at, :].astype(F32)
        first = jnp.mean(dn, axis=1, keepdims=True)
        second = jnp.mean(dn * xhat, axis=1, keepdims=True)
        outs.append((dout + inv * (dn - first - xhat * second)).reshape(16, 8, 768))
    o_ref[...] = jnp.concatenate(outs, axis=1).astype(BF)


def added(refs):
    total = refs[0][...].astype(F32)
    for ref in refs[1:]:
        total = total + ref[...].astype(F32)
    return total.astype(BF)


def split_body(*refs):
    sel = selection(384, split_order())
    for half in range(2):
        out = nn(sel, added(refs[half * 4 : half * 4 + 4])).astype(BF)
        for t in range(4):
            refs[8 + half * 4 + t][...] = out[t * 96 : (t + 1) * 96]


def slot_body(at_ref, back_ref, *refs):
    total = jnp.concatenate([added(refs[0:4]), added(refs[4:8])], axis=0)
    slot, half = slot_order(at_ref[0])
    for h in range(2):
        part = nn(selection(128, jnp.where(half == h, slot, -1)), total).astype(BF)
        refs[8][:, :, h * 384 : (h + 1) * 384] = part.reshape(8, 16, 384)


def home_body(r_ref, ig_ref):
    sel = selection(256, home_order())
    back = lax.dot_general(
        sel, r_ref[...].reshape(256, 768), (((0,), (0,)), ((), ())), preferred_element_type=F32
    )
    ig_ref[...] = back.astype(BF)


def sum_body(at_ref, r_ref, own_ref, oth_ref):
    total = r_ref[0].astype(F32)
    for s in range(1, 8):
        total = total + r_ref[s].astype(F32)
    low = at_ref[0] == 0
    own_ref[...] = jnp.where(low, total[0:8], total[8:16])
    oth_ref[...] = jnp.where(low, total[8:16], total[0:8])


def last_body(at_ref, own_ref, got_ref, gq_ref, go_ref):
    own, got = own_ref[...], got_ref[...]
    low = at_ref[0] == 0
    halves = (jnp.where(low, own, got), jnp.where(low, got, own))
    for h, m in enumerate(halves):
        at = h * 384
        gq_ref[:, at : at + 384] = m[0:3, 0:384]
        gq_ref[:, 768 + at : 768 + at + 384] = m[0:3, 384:768]
        gq_ref[0:1, 1536 + at : 1536 + at + 384] = m[3:4, 0:384]
        gq_ref[1:2, 1536 + at : 1536 + at + 384] = m[3:4, 384:768]
        gq_ref[2:3, 1536 + at : 1536 + at + 384] = m[4:5, 0:384]
    go_ref[...] = own[5:8] + got[5:8]


def local(x, d, w_qkv, w_out):
    at = jnp.stack([lax.axis_index("c"), lax.axis_index("x"), lax.axis_index("y")]).astype(jnp.int32)

    def swap(v):
        return lax.ppermute(v, "c", [(0, 1), (1, 0)])

    def spread(blocks, axis):
        return [blocks[0]] + [
            lax.ppermute(blocks[s], axis, [(i, (i + s) % 4) for i in range(4)]) for s in (2, 1, 3)
        ]

    scr = lambda *s: pltpu.VMEM(s, BF)
    packed, = call(
        pack_body,
        [((16, 32, 768), BF)],
        [x.reshape(256, 768), d.reshape(256, 768)],
        scratch=[scr(256, 768), scr(256, 768), pltpu.SemaphoreType.DMA((2,))],
        hbm=(0, 1),
        limit=63,
    )
    own = lax.all_to_all(packed, ("x", "zh"), split_axis=0, concat_axis=0, tiled=True)
    oth = swap(own)
    dqkv, *grads = call(
        main_body,
        [((512, 1152), BF)] + [((384, 384), BF)] * 8,
        [at, own, oth, w_qkv, w_out],
        scratch=[scr(512, 768), scr(512, 768), scr(512, 1152), scr(512, 384), scr(384, 512),
                 scr(384, 512), scr(384, 512), scr(384, 512), scr(384, 512), scr(768, 512), scr(768, 1152),
                 scr(384, 768), pltpu.SemaphoreType.DMA((4,))],
        smem=(0,),
        hbm=(3, 4),
        limit=58,
        flops=6 * 10**9,
        nbytes=10**7,
    )
    first = spread(grads[:4], "x") + spread(grads[4:], "y")
    mine, theirs = call(
        dnormed_body,
        [((256, 768), F32), ((256, 768), BF)],
        [at, dqkv, w_qkv],
        scratch=[scr(768, 1152), pltpu.SemaphoreType.DMA((3,))],
        smem=(0,),
        hbm=(2,),
        flops=10**9,
        nbytes=5 * 10**6,
        limit=16,
    )
    got = swap(theirs)
    ig, = call(input_gradient_body, [((16, 16, 768), BF)], [mine, got, own], nbytes=3 * 10**6)
    back = lax.all_to_all(ig, ("x", "zh"), split_axis=0, concat_axis=0, tiled=True)
    second = call(split_body, [((96, 384), BF)] * 8, first, flops=4_000_000_000)
    second = spread(second[:4], "y") + spread(second[4:], "x")
    slots, = call(slot_body, [((8, 16, 768), BF)], [at, back, *second], smem=(0,), hbm=(1,))
    ig_home, = call(home_body, [((256, 768), BF)], [back])
    last = lax.all_to_all(slots, ("zh", "zl"), split_axis=0, concat_axis=0, tiled=True)
    own8, oth8 = call(sum_body, [((8, 768), F32)] * 2, [at, last], smem=(0,))
    grad_qkv, grad_out = call(
        last_body, [((3, 2304), F32), ((3, 768), F32)], [at, own8, swap(oth8)], smem=(0,)
    )
    return ig_home.reshape(8, 32, 768), grad_qkv, grad_out


def solution(mesh):
    fine = Mesh(mesh.devices.reshape(4, 4, 2, 2, 4), ("zh", "x", "c", "zl", "y"))
    tm, space = ("zh", "x", "c"), ("zl", "y")
    tokens, rows = P(tm, space, None), P(tm + space, None)
    return jax.shard_map(
        local,
        mesh=fine,
        in_specs=(tokens, tokens, P(), P()),
        out_specs=(tokens, rows, rows),
        check_vma=False,
    )
```

```python
import jax
import jax.numpy as jnp
from jax import lax
from jax.experimental import pallas as pl
from jax.experimental.pallas import tpu as pltpu
from jax.sharding import Mesh, PartitionSpec as P

HEAD = 64
ORDER = ((0, 2), (1, 2), (0, 1), (1, 1), (0, 3), (1, 3))
BF = jnp.bfloat16
F32 = jnp.float32
VM = pl.BlockSpec(memory_space=pltpu.VMEM)
SM = pl.BlockSpec(memory_space=pltpu.SMEM)
HB = pl.BlockSpec(memory_space=pltpu.HBM)


def nn(a, b):
    return lax.dot_general(a, b, (((1,), (0,)), ((), ())), preferred_element_type=F32)


def nt(a, b):
    return lax.dot_general(a, b, (((1,), (1,)), ((), ())), preferred_element_type=F32)


def call(body, outs, ins, scratch=(), smem=(), hbm=(), flops=0, nbytes=0, limit=16):
    space = {i: SM for i in smem} | {i: HB for i in hbm}
    return pl.pallas_call(
        body,
        out_shape=[jax.ShapeDtypeStruct(s, d) for s, d in outs],
        in_specs=[space.get(i, VM) for i in range(len(ins))],
        out_specs=[VM] * len(outs),
        scratch_shapes=list(scratch),
        compiler_params=pltpu.CompilerParams(vmem_limit_bytes=limit * 2**20),
        cost_estimate=pl.CostEstimate(flops=flops, bytes_accessed=nbytes, transcendentals=0),
    )(*ins)


def selection(rows, source):
    at = lax.broadcasted_iota(jnp.int32, (rows, source.shape[1]), 0)
    return (at == source).astype(F32).astype(BF)


def lanes(n):
    return lax.broadcasted_iota(jnp.int32, (1, n), 1)


def third(i):
    return (i * 21846) >> 16


def home_order():
    i = lanes(256)
    f, p = i >> 5, i & 31
    return ((p >> 1) << 4) + ((p & 1) << 3) + f


def feature_order(n, x0, y0):
    f = lanes(n)
    d = third(f)
    c = (d >> 3) & 1
    x, y = (((d >> 4) & 3) - x0) & 3, ((d & 3) - y0) & 3
    first, second = jnp.where(c == 0, x, y), jnp.where(c == 0, y, x)
    low = (d >> 6) * 6 + ((d >> 2) & 1) * 3 + (f - 3 * d)
    return c * (n // 2) + first * (n // 8) + second * (n // 32) + low


def split_order():
    i = lanes(384)
    m = jnp.where(i < 96, 0, jnp.where(i < 192, 1, 2))
    hh = jnp.where(i < 336, 0, 1)
    low, high = i - 96 * m, i - 288 - 48 * hh
    t1 = jnp.where(low < 24, 0, jnp.where(low < 48, 1, jnp.where(low < 72, 2, 3)))
    t2 = jnp.where(high < 12, 0, jnp.where(high < 24, 1, jnp.where(high < 36, 2, 3)))
    return jnp.where(i < 288, t1 * 72 + m * 24 + low, t2 * 84 + 72 + hh * 12 + high)


def slot_order(core):
    i = lanes(192)
    c = jnp.where(i < 96, 0, 1)
    i = i - 96 * c
    big = i < 72
    m = jnp.where(i < 24, 0, jnp.where(i < 48, 1, 2))
    hh = jnp.where(i < 84, 0, 1)
    rem = jnp.where(big, i - 24 * m, i - 72 - 12 * hh)
    d = third(rem)
    j = rem - 3 * d
    row = jnp.where(big, jnp.where(m < 2, j, 3 + (j >> 1)), 5 + j)
    half = jnp.where(big, jnp.where(m < 2, m, j & 1), hh)
    return ((d + jnp.where(big, 0, 4 * core)) << 4) + (c << 3) + row, half


def pack_body(x_ref, d_ref, o_ref, x_s, d_s, sems):
    copies = [pltpu.make_async_copy(r, s, sems.at[i]) for i, (r, s) in enumerate(((x_ref, x_s), (d_ref, d_s)))]
    for copy in copies:
        copy.start()
    sel = selection(256, home_order())
    copies[0].wait()
    o_ref[:, 0:16, :] = nn(sel, x_s[...]).astype(BF).reshape(16, 16, 768)
    copies[1].wait()
    o_ref[:, 16:32, :] = nn(sel, d_s[...]).astype(BF).reshape(16, 16, 768)


def rows_of(ref, first):
    start = first // 16 * 16
    block = ref[:, start : start + 16, :].astype(F32)
    return block[:, first - start : first - start + 8, :].reshape(128, 768)


def normalize(x):
    mean = jnp.mean(x, axis=1, keepdims=True)
    cen = x - mean
    inv = 1.0 / jnp.sqrt(jnp.mean(cen * cen, axis=1, keepdims=True) + 1e-05)
    return cen * inv, inv


def weight_copies(core, source, target, sems):
    copies = []
    for t in range(3):
        cols = pl.ds(pl.multiple_of(t * 768 + core * 384, 128), 384)
        copies.append(pltpu.make_async_copy(source.at[:, cols], target.at[:, t * 384 : (t + 1) * 384], sems.at[t]))
    return copies


def main_body(at_ref, own_ref, oth_ref, wqkv_ref, wout_ref, mine_ref, theirs_ref, xd_ref, *rest):
    g_refs = rest[:7]
    (dqkv_ref, n_s, d_s, qkv_s, a_s, kt_s, vt_s, at_s, dqt_s, att_s, nt_s, w_ref, wo_ref,
     sems) = rest[7:]
    copies = weight_copies(at_ref[0], wqkv_ref, w_ref, sems)
    rows = pl.ds(pl.multiple_of(at_ref[0] * 384, 128), 384)
    copies.append(pltpu.make_async_copy(wout_ref.at[rows, :], wo_ref, sems.at[3]))
    for copy in copies:
        copy.start()
    for patch in range(2):
        for side, ref in enumerate((own_ref, oth_ref)):
            at = patch * 256 + side * 128
            x, d = rows_of(ref, patch * 8), rows_of(ref, 16 + patch * 8).astype(BF)
            n_s[at : at + 128, :] = normalize(x)[0].astype(BF)
            d_s[at : at + 128, :] = d
            if side == 0:
                xd_ref[patch * 128 : patch * 128 + 128, :] = x.astype(BF)
                xd_ref[256 + patch * 128 : 256 + patch * 128 + 128, :] = d
    for t in range(3):
        copies[t].wait()
        qkv_s[:, t * 384 : (t + 1) * 384] = nn(n_s[...], w_ref[:, t * 384 : (t + 1) * 384]).astype(BF)
    copies[3].wait()
    a_s[...] = nt(d_s[...], wo_ref[...]).astype(BF)
    kt_s[...] = (qkv_s[:, 384:768] * 0.125).T
    vt_s[...] = qkv_s[:, 768:1152].T
    at_s[...] = a_s[...].T
    lane = lax.broadcasted_iota(jnp.int32, (1, 128), 1)

    keeps = [((lane >= h * HEAD) & (lane < (h + 1) * HEAD)).astype(F32).astype(BF) for h in range(2)]
    work = []
    for pair in range(3):
        for patch in range(2):
            rows, at = slice(patch * 256, (patch + 1) * 256), pair * 128
            q = qkv_s[rows, at : at + 128] * 0.125
            k = qkv_s[rows, 384 + at : 384 + at + 128]
            v = qkv_s[rows, 768 + at : 768 + at + 128]
            a = a_s[rows, at : at + 128]
            for h in range(2):
                work.append((rows, at, slice(at + h * HEAD, at + (h + 1) * HEAD), q * keeps[h], a * keeps[h], k, v))
    sts = [nt(k, qh) for _, _, _, qh, _, k, _ in work]
    dps = [nt(v, ah) for _, _, _, _, ah, _, v in work]
    ps = []
    for st in sts:
        e = jnp.exp(st - jnp.max(st, axis=0, keepdims=True))
        ps.append(e * (1.0 / jnp.sum(e, axis=0, keepdims=True)))
    pbs = [p.astype(BF) for p in ps]
    dss = []
    for (rows, _, hr, _, _, _, _), p, pb, dp in zip(work, ps, pbs, dps):
        attn = nn(vt_s[hr, rows], pb).astype(BF)
        att_s[hr, rows] = attn
        delta = jnp.sum(at_s[hr, rows].astype(F32) * attn.astype(F32), axis=0, keepdims=True)
        dss.append((p * (dp - delta)).astype(BF))
    for i in range(0, 12, 2):
        rows, at = work[i][:2]
        dv = nn(pbs[i], work[i][4]) + nn(pbs[i + 1], work[i + 1][4])
        dk = nn(dss[i], work[i][3]) + nn(dss[i + 1], work[i + 1][3])
        dqkv_ref[rows, 768 + at : 768 + at + 128] = dv.astype(BF)
        dqkv_ref[rows, 384 + at : 384 + at + 128] = dk.astype(BF)
    for (rows, _, hr, _, _, _, _), ds in zip(work, dss):
        dqt_s[hr, rows] = nn(kt_s[hr, rows], ds).astype(BF)
    dqkv_ref[:, 0:384] = dqt_s[...].T
    part = nt(dqkv_ref[...], w_ref[...])
    for patch in range(2):
        mine_ref[patch * 128 : (patch + 1) * 128, :] = part[patch * 256 : patch * 256 + 128]
        theirs_ref[patch * 128 : (patch + 1) * 128, :] = part[patch * 256 + 128 : patch * 256 + 256].astype(BF)

    def put(i, row, value):
        half, s = divmod(i, 4)
        ref, row = (g_refs[6], half * 384 + row) if s == 0 else (g_refs[half * 3 + s - 1], row)
        ref[row : row + value.shape[0], :] = value

    nt_s[...] = nt(selection(768, feature_order(768, at_ref[1], at_ref[2])), n_s[...]).astype(BF)
    for t in range(3):
        g = nn(nt_s[...], dqkv_ref[:, t * 384 : (t + 1) * 384]).astype(BF)
        for i in range(8):
            put(i, t * 96, g[i * 96 : (i + 1) * 96])
    attp = nn(selection(384, feature_order(384, at_ref[1], at_ref[2])), att_s[...]).astype(BF)
    for t in range(2):
        g = nn(attp, d_s[:, t * 384 : (t + 1) * 384]).astype(BF)
        for i in range(8):
            put(i, 288 + t * 48, g[i * 48 : (i + 1) * 48])


def input_gradient_body(part_ref, got_ref, xd_ref, o_ref):
    outs = []
    for patch in range(2):
        xhat, inv = normalize(xd_ref[patch * 128 : patch * 128 + 128, :].astype(F32))
        dout = xd_ref[256 + patch * 128 : 256 + patch * 128 + 128, :].astype(F32)
        at = pl.ds(patch * 128, 128)
        dn = part_ref[at, :] + got_ref[at, :].astype(F32)
        first = jnp.mean(dn, axis=1, keepdims=True)
        second = jnp.mean(dn * xhat, axis=1, keepdims=True)
        outs.append((dout + inv * (dn - first - xhat * second)).reshape(16, 8, 768))
    o_ref[...] = jnp.concatenate(outs, axis=1).astype(BF)


def added(refs, half):
    rows = refs[6].shape[0] // 2
    total = refs[6][half * rows : (half + 1) * rows].astype(F32)
    for (i, _), ref in zip(ORDER, refs):
        if i == half:
            total = total + ref[...].astype(F32)
    return total.astype(BF)


def split_body(*refs):
    sel = selection(384, split_order())
    for half in range(2):
        out = nn(sel, added(refs, half)).astype(BF)
        refs[13][half * 96 : half * 96 + 96] = out[0:96]
        for t in range(3):
            refs[7 + half * 3 + t][...] = out[(t + 1) * 96 : (t + 2) * 96]


def slot_body(at_ref, done_ref, *refs):
    total = jnp.concatenate([added(refs, 0), added(refs, 1)], axis=0)
    slot, half = slot_order(at_ref[0])
    for h in range(2):
        part = nn(selection(128, jnp.where(half == h, slot, -1)), total).astype(BF)
        refs[7][:, :, h * 384 : (h + 1) * 384] = part.reshape(16, 8, 384)


def home_body(r_ref, ig_ref, done_ref):
    sel = selection(256, home_order())
    back = lax.dot_general(
        sel, r_ref[...].reshape(256, 768), (((0,), (0,)), ((), ())), preferred_element_type=F32
    )
    ig_ref[...] = back.astype(BF)
    done_ref[...] = jnp.zeros_like(done_ref)


def last_body(r_ref, gq_ref, go_ref):
    halves = []
    for h in range(2):
        total = r_ref[h].astype(F32)
        for z in range(1, 8):
            total = total + r_ref[2 * z + h].astype(F32)
        halves.append(total)
    for h, m in enumerate(halves):
        at = h * 384
        gq_ref[:, at : at + 384] = m[0:3, 0:384]
        gq_ref[:, 768 + at : 768 + at + 384] = m[0:3, 384:768]
        gq_ref[0:1, 1536 + at : 1536 + at + 384] = m[3:4, 0:384]
        gq_ref[1:2, 1536 + at : 1536 + at + 384] = m[3:4, 384:768]
        gq_ref[2:3, 1536 + at : 1536 + at + 384] = m[4:5, 0:384]
    go_ref[...] = halves[0][5:8] + halves[1][5:8]


def local(x, d, w_qkv, w_out):
    at = jnp.stack([lax.axis_index("c"), lax.axis_index("x"), lax.axis_index("y")]).astype(jnp.int32)

    def swap(v):
        return lax.ppermute(v, "c", [(0, 1), (1, 0)])

    def spread(blocks, axes):
        moved = [
            lax.ppermute(blocks[i * 3 + s - 1], axes[i], [(j, (j + s) % 4) for j in range(4)]) for i, s in ORDER
        ]
        return moved + [blocks[6]]

    scr = lambda *s: pltpu.VMEM(s, BF)
    packed, = call(
        pack_body,
        [((16, 32, 768), BF)],
        [x.reshape(256, 768), d.reshape(256, 768)],
        scratch=[scr(256, 768), scr(256, 768), pltpu.SemaphoreType.DMA((2,))],
        hbm=(0, 1),
        limit=63,
    )
    own = lax.all_to_all(packed, ("x", "zh"), split_axis=0, concat_axis=0, tiled=True)
    oth = swap(own)
    mine, theirs, xd, *grads = call(
        main_body,
        [((256, 768), F32), ((256, 768), BF), ((512, 768), BF)] + [((384, 384), BF)] * 6 + [((768, 384), BF)],
        [at, own, oth, w_qkv, w_out],
        scratch=[scr(512, 1152), scr(512, 768), scr(512, 768), scr(512, 1152), scr(512, 384), scr(384, 512),
                 scr(384, 512), scr(384, 512), scr(384, 512), scr(384, 512), scr(768, 512), scr(768, 1152),
                 scr(384, 768), pltpu.SemaphoreType.DMA((4,))],
        smem=(0,),
        hbm=(3, 4),
        limit=50,
        flops=6 * 10**9,
        nbytes=10**7,
    )
    first = spread(grads, "xy")
    got = swap(theirs)
    ig, = call(input_gradient_body, [((16, 16, 768), BF)], [mine, got, xd], nbytes=3 * 10**6)
    back = lax.all_to_all(ig, ("x", "zh"), split_axis=0, concat_axis=0, tiled=True)
    second = call(split_body, [((96, 384), BF)] * 6 + [((192, 384), BF)], first, flops=4_000_000_000)
    second = spread(second, "yx")
    ig_home, done = call(home_body, [((256, 768), BF), ((8, 128), F32)], [back])
    slots, = call(slot_body, [((16, 8, 768), BF)], [at, done, *second], smem=(0,))
    last = lax.all_to_all(slots, ("zh", "zl", "c"), split_axis=0, concat_axis=0, tiled=True)
    grad_qkv, grad_out = call(last_body, [((3, 2304), F32), ((3, 768), F32)], [last])
    return ig_home.reshape(8, 32, 768), grad_qkv, grad_out


def solution(mesh):
    fine = Mesh(mesh.devices.reshape(4, 4, 2, 2, 4), ("zh", "x", "c", "zl", "y"))
    tm, space = ("zh", "x", "c"), ("zl", "y")
    tokens, rows = P(tm, space, None), P(tm + space, None)
    return jax.shard_map(
        local,
        mesh=fine,
        in_specs=(tokens, tokens, P(), P()),
        out_specs=(tokens, rows, rows),
        check_vma=False,
    )
```

```python
import jax
import jax.numpy as jnp
from jax import lax
from jax.experimental import pallas as pl
from jax.experimental.pallas import tpu as pltpu
from jax.sharding import Mesh, PartitionSpec as P

HEAD = 64
BF = jnp.bfloat16
F32 = jnp.float32
VM = pl.BlockSpec(memory_space=pltpu.VMEM)
SM = pl.BlockSpec(memory_space=pltpu.SMEM)
HB = pl.BlockSpec(memory_space=pltpu.HBM)


def nn(a, b):
    return lax.dot_general(a, b, (((1,), (0,)), ((), ())), preferred_element_type=F32)


def nt(a, b):
    return lax.dot_general(a, b, (((1,), (1,)), ((), ())), preferred_element_type=F32)


def call(body, outs, ins, scratch=(), smem=(), hbm=(), passed=None, flops=0, nbytes=0, limit=8):
    passed = passed or {}
    space = {i: SM for i in smem} | {i: HB for i in (*hbm, *passed)}
    return pl.pallas_call(
        body,
        out_shape=[jax.ShapeDtypeStruct(s, d) for s, d in outs],
        in_specs=[space.get(i, VM) for i in range(len(ins))],
        out_specs=[HB if i in passed.values() else VM for i in range(len(outs))],
        input_output_aliases=passed,
        scratch_shapes=list(scratch),
        compiler_params=pltpu.CompilerParams(vmem_limit_bytes=limit * 2**20),
        cost_estimate=pl.CostEstimate(flops=flops, bytes_accessed=nbytes, transcendentals=0),
    )(*ins)


def selection(rows, source):
    at = lax.broadcasted_iota(jnp.int32, (rows, source.shape[1]), 0)
    return (at == source).astype(F32).astype(BF)


def lanes(n):
    return lax.broadcasted_iota(jnp.int32, (1, n), 1)


def third(i):
    return (i * 21846) >> 16


def home_order():
    i = lanes(256)
    f, p = i >> 5, i & 31
    return ((p >> 1) << 4) + ((p & 1) << 3) + f


def feature_order(n, role, x0, y0):
    f = lanes(n)
    d = third(f)
    c = (d >> 3) & 1
    x, y = (((d >> 4) & 3) - x0) & 3, ((d & 3) - y0) & 3
    first, second = jnp.where(c == 0, x, y), jnp.where(c == 0, y, x)
    low = (d >> 6) * 6 + ((d >> 2) & 1) * 3 + (f - 3 * d)
    return (c ^ role) * (n // 2) + first * (n // 8) + second * (n // 32) + low


def split_order():
    i = lanes(384)
    m = jnp.where(i < 96, 0, jnp.where(i < 192, 1, 2))
    hh = jnp.where(i < 336, 0, 1)
    low, high = i - 96 * m, i - 288 - 48 * hh
    t1 = jnp.where(low < 24, 0, jnp.where(low < 48, 1, jnp.where(low < 72, 2, 3)))
    t2 = jnp.where(high < 12, 0, jnp.where(high < 24, 1, jnp.where(high < 36, 2, 3)))
    return jnp.where(i < 288, t1 * 72 + m * 24 + low, t2 * 84 + 72 + hh * 12 + high)


def slot_order():
    i = lanes(192)
    k = jnp.where(i < 96, 0, 1)
    i = i - 96 * k
    big = i < 72
    m = jnp.where(i < 24, 0, jnp.where(i < 48, 1, 2))
    hh = jnp.where(i < 84, 0, 1)
    rem = jnp.where(big, i - 24 * m, i - 72 - 12 * hh)
    d = third(rem)
    j = rem - 3 * d
    row = jnp.where(big, jnp.where(m < 2, j, 3 + (j >> 1)), 5 + j)
    half = jnp.where(big, jnp.where(m < 2, m, j & 1), hh)
    return ((d + jnp.where(big, 0, 4 * k)) << 4) + (k << 3) + row, half


def pack_body(x_ref, d_ref, o_ref, x_s, d_s, sems):
    copies = [pltpu.make_async_copy(r, s, sems.at[i]) for i, (r, s) in enumerate(((x_ref, x_s), (d_ref, d_s)))]
    for copy in copies:
        copy.start()
    sel = selection(256, home_order())
    copies[0].wait()
    o_ref[:, 0:16, :] = nn(sel, x_s[...]).astype(BF).reshape(16, 16, 768)
    copies[1].wait()
    o_ref[:, 16:32, :] = nn(sel, d_s[...]).astype(BF).reshape(16, 16, 768)


def rows_of(ref, first):
    start = first // 16 * 16
    block = ref[:, start : start + 16, :].astype(F32)
    return block[:, first - start : first - start + 8, :].reshape(128, 768)


def normalize(x):
    mean = jnp.mean(x, axis=1, keepdims=True)
    cen = x - mean
    inv = 1.0 / jnp.sqrt(jnp.mean(cen * cen, axis=1, keepdims=True) + 1e-05)
    return cen * inv, inv


def weight_copies(core, source, target, sems):
    copies = []
    for t in range(3):
        cols = pl.ds(pl.multiple_of(t * 768 + core * 384, 128), 384)
        copies.append(pltpu.make_async_copy(source.at[:, cols], target.at[:, t * 384 : (t + 1) * 384], sems.at[t]))
    return copies


def tokens_of(ref):
    x, d = ([rows_of(ref, first + patch * 8) for patch in range(2)] for first in (0, 16))
    return jnp.concatenate(x, axis=0), jnp.concatenate(d, axis=0).astype(BF)


def own_body(at_ref, own_ref, wqkv_ref, wout_ref, xd_ref, qkv_ref, a_ref, nt_ref, w_ref, wo_ref, sems):
    copies = weight_copies(at_ref[0], wqkv_ref, w_ref, sems)
    rows = pl.ds(pl.multiple_of(at_ref[0] * 384, 128), 384)
    copies.append(pltpu.make_async_copy(wout_ref.at[rows, :], wo_ref, sems.at[3]))
    for copy in copies:
        copy.start()
    x, d = tokens_of(own_ref)
    xd_ref[0:256, :] = x.astype(BF)
    xd_ref[256:512, :] = d
    n = normalize(x)[0].astype(BF)
    nt_ref[...] = nt(selection(768, feature_order(768, at_ref[3], at_ref[1], at_ref[2])), n).astype(BF)
    for t in range(3):
        copies[t].wait()
        qkv_ref[:, t * 384 : (t + 1) * 384] = nn(n, w_ref[:, t * 384 : (t + 1) * 384]).astype(BF)
    copies[3].wait()
    a_ref[...] = nt(d, wo_ref[...]).astype(BF)


def main_body(at_ref, oth_ref, xd_ref, qkv0_ref, a0_ref, nt0_ref, w_ref, wo_ref, mine_ref, theirs_ref, *rest):
    stay_refs, go_ref = rest[:4], rest[4]
    dqkv_ref, d_s, qkv_s, a_s, kt_s, vt_s, at_s, dqt_s, att_s, nt_s = rest[5:]
    x, d = tokens_of(oth_ref)
    n = normalize(x)[0].astype(BF)
    nt1 = nt(selection(768, feature_order(768, at_ref[3], at_ref[1], at_ref[2])), n).astype(BF)
    a1 = nt(d, wo_ref[...]).astype(BF)
    qkv1 = [nn(n, w_ref[:, t * 384 : (t + 1) * 384]).astype(BF) for t in range(3)]
    for patch in range(2):
        here = slice(patch * 128, (patch + 1) * 128)
        one, two = (slice(patch * 256 + side * 128, patch * 256 + side * 128 + 128) for side in range(2))
        qkv_s[one, :], a_s[one, :], nt_s[:, one] = qkv0_ref[here, :], a0_ref[here, :], nt0_ref[:, here]
        d_s[one, :] = xd_ref[256 + patch * 128 : 384 + patch * 128, :]
        a_s[two, :], nt_s[:, two], d_s[two, :] = a1[here], nt1[:, here], d[here]
        for t in range(3):
            qkv_s[two, t * 384 : (t + 1) * 384] = qkv1[t][here]
    kt_s[...] = (qkv_s[:, 384:768] * 0.125).T
    vt_s[...] = qkv_s[:, 768:1152].T
    at_s[...] = a_s[...].T
    lane = lax.broadcasted_iota(jnp.int32, (1, 128), 1)

    keeps = [((lane >= h * HEAD) & (lane < (h + 1) * HEAD)).astype(F32).astype(BF) for h in range(2)]
    work = []
    for pair in range(3):
        for patch in range(2):
            rows, at = slice(patch * 256, (patch + 1) * 256), pair * 128
            q = qkv_s[rows, at : at + 128] * 0.125
            k = qkv_s[rows, 384 + at : 384 + at + 128]
            v = qkv_s[rows, 768 + at : 768 + at + 128]
            a = a_s[rows, at : at + 128]
            for h in range(2):
                work.append((rows, at, slice(at + h * HEAD, at + (h + 1) * HEAD), q * keeps[h], a * keeps[h], k, v))
    sts = [nt(k, qh) for _, _, _, qh, _, k, _ in work]
    dps = [nt(v, ah) for _, _, _, _, ah, _, v in work]
    ps = []
    for st in sts:
        e = jnp.exp(st - jnp.max(st, axis=0, keepdims=True))
        ps.append(e * (1.0 / jnp.sum(e, axis=0, keepdims=True)))
    pbs = [p.astype(BF) for p in ps]
    dss = []
    for (rows, _, hr, _, _, _, _), p, pb, dp in zip(work, ps, pbs, dps):
        attn = nn(vt_s[hr, rows], pb).astype(BF)
        att_s[hr, rows] = attn
        delta = jnp.sum(at_s[hr, rows].astype(F32) * attn.astype(F32), axis=0, keepdims=True)
        dss.append((p * (dp - delta)).astype(BF))
    for i in range(0, 12, 2):
        rows, at = work[i][:2]
        dv = nn(pbs[i], work[i][4]) + nn(pbs[i + 1], work[i + 1][4])
        dk = nn(dss[i], work[i][3]) + nn(dss[i + 1], work[i + 1][3])
        dqkv_ref[rows, 768 + at : 768 + at + 128] = dv.astype(BF)
        dqkv_ref[rows, 384 + at : 384 + at + 128] = dk.astype(BF)
    for (rows, _, hr, _, _, _, _), ds in zip(work, dss):
        dqt_s[hr, rows] = nn(kt_s[hr, rows], ds).astype(BF)
    dqkv_ref[:, 0:384] = dqt_s[...].T
    part = nt(dqkv_ref[...], w_ref[...])
    for patch in range(2):
        mine_ref[patch * 128 : (patch + 1) * 128, :] = part[patch * 256 : patch * 256 + 128]
        theirs_ref[patch * 128 : (patch + 1) * 128, :] = part[patch * 256 + 128 : patch * 256 + 256].astype(BF)

    def put(i, row, value):
        ref, row = (stay_refs[i], row) if i < 4 else (go_ref, (i - 4) * 384 + row)
        ref[row : row + value.shape[0], :] = value

    for t in range(3):
        g = nn(nt_s[...], dqkv_ref[:, t * 384 : (t + 1) * 384]).astype(BF)
        for i in range(8):
            put(i, t * 96, g[i * 96 : (i + 1) * 96])
    attp = nn(selection(384, feature_order(384, at_ref[3], at_ref[1], at_ref[2])), att_s[...]).astype(BF)
    for t in range(2):
        g = nn(attp, d_s[:, t * 384 : (t + 1) * 384]).astype(BF)
        for i in range(8):
            put(i, 288 + t * 48, g[i * 48 : (i + 1) * 48])


def input_gradient_body(part_ref, got_ref, xd_ref, blocks_ref, keep_ref, o_ref, same_ref, *block_refs):
    for s in range(4):
        block_refs[s][...] = blocks_ref[s * 384 : (s + 1) * 384]
    outs = []
    for patch in range(2):
        xhat, inv = normalize(xd_ref[patch * 128 : patch * 128 + 128, :].astype(F32))
        dout = xd_ref[256 + patch * 128 : 256 + patch * 128 + 128, :].astype(F32)
        at = pl.ds(patch * 128, 128)
        dn = part_ref[at, :] + got_ref[at, :].astype(F32)
        first = jnp.mean(dn, axis=1, keepdims=True)
        second = jnp.mean(dn * xhat, axis=1, keepdims=True)
        outs.append((dout + inv * (dn - first - xhat * second)).reshape(16, 8, 768))
    o_ref[...] = jnp.concatenate(outs, axis=1).astype(BF)


def added(refs):
    total = refs[0][...].astype(F32)
    for ref in refs[1:]:
        total = total + ref[...].astype(F32)
    return total.astype(BF)


def split_body(at_ref, *refs):
    sel = selection(384, split_order())
    for k in range(2):
        total = added([refs[2 * i + (k ^ (step & 1))] for i, step in enumerate((2, 1, 3, 0))])
        out = nn(sel, total).astype(BF)
        rows = pl.ds((at_ref[0] ^ k) * 96, 96)
        for t in range(4):
            refs[8 + t][rows] = out[t * 96 : (t + 1) * 96]


def slot_body(done_ref, *refs):
    total = added(refs[:4])
    slot, half = slot_order()
    for h in range(2):
        part = nn(selection(128, jnp.where(half == h, slot, -1)), total).astype(BF)
        refs[4][:, :, h * 384 : (h + 1) * 384] = part.reshape(8, 16, 384)


def home_body(r_ref, ig_ref, done_ref):
    sel = selection(256, home_order())
    back = lax.dot_general(
        sel, r_ref[...].reshape(256, 768), (((0,), (0,)), ((), ())), preferred_element_type=F32
    )
    ig_ref[...] = back.astype(BF)
    done_ref[...] = jnp.zeros_like(done_ref)


def last_body(r_ref, gq_ref, go_ref):
    total = r_ref[0].astype(F32)
    for z in range(1, 8):
        total = total + r_ref[z].astype(F32)
    halves = total[0:8], total[8:16]
    for h, m in enumerate(halves):
        at = h * 384
        gq_ref[:, at : at + 384] = m[0:3, 0:384]
        gq_ref[:, 768 + at : 768 + at + 384] = m[0:3, 384:768]
        gq_ref[0:1, 1536 + at : 1536 + at + 384] = m[3:4, 0:384]
        gq_ref[1:2, 1536 + at : 1536 + at + 384] = m[3:4, 384:768]
        gq_ref[2:3, 1536 + at : 1536 + at + 384] = m[4:5, 0:384]
    go_ref[...] = halves[0][5:8] + halves[1][5:8]


def local(x, d, w_qkv, w_out):
    core, x0, y0 = (lax.axis_index(a) for a in ("c", "x", "y"))
    role = core ^ ((x0 + y0) & 1)
    at = jnp.stack([core, x0, y0, role]).astype(jnp.int32)

    def swap(v):
        return lax.ppermute(v, "c", [(0, 1), (1, 0)])

    def spread(blocks, axes, steps, home):
        moved = []
        for s in steps:
            pairs = []
            for x in range(4):
                for y in range(4):
                    for k in range(2):
                        u, v = ((x + s) % 4, y) if axes[k] == "x" else (x, (y + s) % 4)
                        c, d = k ^ ((x + y) & 1), k if home else k ^ ((u + v) & 1)
                        pairs.append(((x * 2 + c) * 4 + y, (u * 2 + d) * 4 + v))
            each = len(blocks) // 4
            for block in blocks[s * each : s * each + each]:
                moved.append(lax.ppermute(block, ("x", "c", "y"), pairs))
        return moved

    scr = lambda *s: pltpu.VMEM(s, BF)
    packed, = call(
        pack_body,
        [((16, 32, 768), BF)],
        [x.reshape(256, 768), d.reshape(256, 768)],
        scratch=[scr(256, 768), scr(256, 768), pltpu.SemaphoreType.DMA((2,))],
        hbm=(0, 1),
        limit=60,
    )
    own = lax.all_to_all(packed, ("x", "zh"), split_axis=0, concat_axis=0, tiled=True)
    oth = swap(own)
    xd, *projected = call(
        own_body,
        [((512, 768), BF), ((256, 1152), BF), ((256, 384), BF), ((768, 256), BF), ((768, 1152), BF), ((384, 768), BF)],
        [at, own, w_qkv, w_out],
        scratch=[pltpu.SemaphoreType.DMA((4,))],
        smem=(0,),
        hbm=(2, 3),
        flops=10**9,
        nbytes=5 * 10**6,
        limit=46,
    )
    mine, theirs, *grads = call(
        main_body,
        [((256, 768), F32), ((256, 768), BF)] + [((384, 384), BF)] * 4 + [((1536, 384), BF)],
        [at, oth, xd, *projected],
        scratch=[scr(512, 1152), scr(512, 768), scr(512, 1152), scr(512, 384), scr(384, 512), scr(384, 512),
                 scr(384, 512), scr(384, 512), scr(384, 512), scr(768, 512)],
        smem=(0,),
        limit=32,
        flops=5 * 10**9,
        nbytes=10**7,
    )
    got = swap(theirs)
    ig, keep, *others = call(
        input_gradient_body,
        [((16, 16, 768), BF)] + [((384, 384), BF)] * 5,
        [mine, got, xd, swap(grads[4]), grads[0]],
        passed={4: 1},
        nbytes=3 * 10**6,
    )
    first = spread([b for pair in zip(grads[:4], others) for b in pair], "xy", (2, 1, 3), False) + [keep, others[0]]
    back = lax.all_to_all(ig, ("x", "zh"), split_axis=0, concat_axis=0, tiled=True)
    second = call(split_body, [((192, 384), BF)] * 4, [at, *first], smem=(0,), flops=4_000_000_000)
    second = spread(second, "yx", (2, 1, 3, 0), True)
    ig_home, done = call(home_body, [((256, 768), BF), ((8, 128), F32)], [back])
    slots, = call(slot_body, [((8, 16, 768), BF)], [done, *second])
    last = lax.all_to_all(slots, ("zh", "zl"), split_axis=0, concat_axis=0, tiled=True)
    grad_qkv, grad_out = call(last_body, [((3, 2304), F32), ((3, 768), F32)], [last])
    return ig_home.reshape(8, 32, 768), grad_qkv, grad_out


def solution(mesh):
    fine = Mesh(mesh.devices.reshape(4, 4, 2, 2, 4), ("zh", "x", "c", "zl", "y"))
    tm, space = ("zh", "x", "c"), ("zl", "y")
    tokens, rows = P(tm, space, None), P(tm + space, None)
    return jax.shard_map(
        local,
        mesh=fine,
        in_specs=(tokens, tokens, P(), P()),
        out_specs=(tokens, rows, rows),
        check_vma=False,
    )
```

```python
import jax
import jax.numpy as jnp
from jax import lax
from jax.experimental import pallas as pl
from jax.experimental.pallas import tpu as pltpu
from jax.sharding import Mesh, PartitionSpec as P

HEAD = 64
BF = jnp.bfloat16
F32 = jnp.float32
VM = pl.BlockSpec(memory_space=pltpu.VMEM)
SM = pl.BlockSpec(memory_space=pltpu.SMEM)
HB = pl.BlockSpec(memory_space=pltpu.HBM)


def nn(a, b):
    return lax.dot_general(a, b, (((1,), (0,)), ((), ())), preferred_element_type=F32)


def nt(a, b):
    return lax.dot_general(a, b, (((1,), (1,)), ((), ())), preferred_element_type=F32)


def call(body, outs, ins, scratch=(), smem=(), hbm=(), passed=None, flops=0, nbytes=0, limit=8):
    passed = passed or {}
    space = {i: SM for i in smem} | {i: HB for i in (*hbm, *passed)}
    return pl.pallas_call(
        body,
        out_shape=[jax.ShapeDtypeStruct(s, d) for s, d in outs],
        in_specs=[space.get(i, VM) for i in range(len(ins))],
        out_specs=[HB if i in passed.values() else VM for i in range(len(outs))],
        input_output_aliases=passed,
        scratch_shapes=list(scratch),
        compiler_params=pltpu.CompilerParams(vmem_limit_bytes=limit * 2**20),
        cost_estimate=pl.CostEstimate(flops=flops, bytes_accessed=nbytes, transcendentals=0),
    )(*ins)


def selection(rows, source):
    at = lax.broadcasted_iota(jnp.int32, (rows, source.shape[1]), 0)
    return (at == source).astype(F32).astype(BF)


def lanes(n):
    return lax.broadcasted_iota(jnp.int32, (1, n), 1)


def third(i):
    return (i * 21846) >> 16


def home_order():
    i = lanes(256)
    f, p = i >> 5, i & 31
    return ((p >> 1) << 4) + ((p & 1) << 3) + f


def feature_order(n, role, x0, y0):
    f = lanes(n)
    d = third(f)
    c = (d >> 3) & 1
    x, y = (((d >> 4) & 3) - x0) & 3, ((d & 3) - y0) & 3
    first, second = jnp.where(c == 0, x, y), jnp.where(c == 0, y, x)
    low = (d >> 6) * 6 + ((d >> 2) & 1) * 3 + (f - 3 * d)
    return (c ^ role) * (n // 2) + first * (n // 8) + second * (n // 32) + low


def split_order():
    i = lanes(384)
    m = jnp.where(i < 96, 0, jnp.where(i < 192, 1, 2))
    hh = jnp.where(i < 336, 0, 1)
    low, high = i - 96 * m, i - 288 - 48 * hh
    t1 = jnp.where(low < 24, 0, jnp.where(low < 48, 1, jnp.where(low < 72, 2, 3)))
    t2 = jnp.where(high < 12, 0, jnp.where(high < 24, 1, jnp.where(high < 36, 2, 3)))
    return jnp.where(i < 288, t1 * 72 + m * 24 + low, t2 * 84 + 72 + hh * 12 + high)


def slot_order():
    i = lanes(192)
    k = jnp.where(i < 96, 0, 1)
    i = i - 96 * k
    big = i < 72
    m = jnp.where(i < 24, 0, jnp.where(i < 48, 1, 2))
    hh = jnp.where(i < 84, 0, 1)
    rem = jnp.where(big, i - 24 * m, i - 72 - 12 * hh)
    d = third(rem)
    j = rem - 3 * d
    row = jnp.where(big, jnp.where(m < 2, j, 3 + (j >> 1)), 5 + j)
    half = jnp.where(big, jnp.where(m < 2, m, j & 1), hh)
    d = d + jnp.where(big, 0, 4 * k)
    slot = ((d & 1) << 2) + (d & 2) + (d >> 2)
    return (slot << 4) + (k << 3) + row, half


def pack_body(x_ref, d_ref, o_ref, x_s, d_s, sems):
    copies = [pltpu.make_async_copy(r, s, sems.at[i]) for i, (r, s) in enumerate(((x_ref, x_s), (d_ref, d_s)))]
    for copy in copies:
        copy.start()
    sel = selection(256, home_order())
    copies[0].wait()
    o_ref[:, 0:16, :] = nn(sel, x_s[...]).astype(BF).reshape(16, 16, 768)
    copies[1].wait()
    o_ref[:, 16:32, :] = nn(sel, d_s[...]).astype(BF).reshape(16, 16, 768)


def rows_of(ref, first):
    start = first // 16 * 16
    block = ref[:, start : start + 16, :].astype(F32)
    return block[:, first - start : first - start + 8, :].reshape(128, 768)


def normalize(x):
    mean = jnp.mean(x, axis=1, keepdims=True)
    cen = x - mean
    inv = 1.0 / jnp.sqrt(jnp.mean(cen * cen, axis=1, keepdims=True) + 1e-05)
    return cen * inv, inv


def weight_copies(core, source, target, sems):
    copies = []
    for t in range(3):
        cols = pl.ds(pl.multiple_of(t * 768 + core * 384, 128), 384)
        copies.append(pltpu.make_async_copy(source.at[:, cols], target.at[:, t * 384 : (t + 1) * 384], sems.at[t]))
    return copies


def tokens_of(ref):
    x, d = ([rows_of(ref, first + patch * 8) for patch in range(2)] for first in (0, 16))
    return jnp.concatenate(x, axis=0), jnp.concatenate(d, axis=0).astype(BF)


def own_body(at_ref, own_ref, wqkv_ref, wout_ref, xd_ref, qkv_ref, a_ref, nt_ref, w_ref, wo_ref, sems):
    copies = weight_copies(at_ref[0], wqkv_ref, w_ref, sems)
    rows = pl.ds(pl.multiple_of(at_ref[0] * 384, 128), 384)
    copies.append(pltpu.make_async_copy(wout_ref.at[rows, :], wo_ref, sems.at[3]))
    for copy in copies:
        copy.start()
    x, d = tokens_of(own_ref)
    xd_ref[0:256, :] = x.astype(BF)
    xd_ref[256:512, :] = d
    n = normalize(x)[0].astype(BF)
    nt_ref[...] = nt(selection(768, feature_order(768, at_ref[3], at_ref[1], at_ref[2])), n).astype(BF)
    for t in range(3):
        copies[t].wait()
        qkv_ref[:, t * 384 : (t + 1) * 384] = nn(n, w_ref[:, t * 384 : (t + 1) * 384]).astype(BF)
    copies[3].wait()
    a_ref[...] = nt(d, wo_ref[...]).astype(BF)


def main_body(at_ref, oth_ref, xd_ref, qkv0_ref, a0_ref, nt0_ref, w_ref, wo_ref, mine_ref, theirs_ref, *rest):
    stay_refs, go_ref = rest[:4], rest[4]
    dqkv_ref, d_s, qkv_s, a_s, kt_s, vt_s, at_s, dqt_s, att_s, nt_s = rest[5:]
    x, d = tokens_of(oth_ref)
    n = normalize(x)[0].astype(BF)
    nt1 = nt(selection(768, feature_order(768, at_ref[3], at_ref[1], at_ref[2])), n).astype(BF)
    a1 = nt(d, wo_ref[...]).astype(BF)
    qkv1 = [nn(n, w_ref[:, t * 384 : (t + 1) * 384]).astype(BF) for t in range(3)]
    for patch in range(2):
        here = slice(patch * 128, (patch + 1) * 128)
        one, two = (slice(patch * 256 + side * 128, patch * 256 + side * 128 + 128) for side in range(2))
        qkv_s[one, :], a_s[one, :], nt_s[:, one] = qkv0_ref[here, :], a0_ref[here, :], nt0_ref[:, here]
        d_s[one, :] = xd_ref[256 + patch * 128 : 384 + patch * 128, :]
        a_s[two, :], nt_s[:, two], d_s[two, :] = a1[here], nt1[:, here], d[here]
        for t in range(3):
            qkv_s[two, t * 384 : (t + 1) * 384] = qkv1[t][here]
    kt_s[...] = (qkv_s[:, 384:768] * 0.125).T
    vt_s[...] = qkv_s[:, 768:1152].T
    at_s[...] = a_s[...].T
    lane = lax.broadcasted_iota(jnp.int32, (1, 128), 1)

    keeps = [((lane >= h * HEAD) & (lane < (h + 1) * HEAD)).astype(F32).astype(BF) for h in range(2)]
    work = []
    for pair in range(3):
        for patch in range(2):
            rows, at = slice(patch * 256, (patch + 1) * 256), pair * 128
            q = qkv_s[rows, at : at + 128] * 0.125
            k = qkv_s[rows, 384 + at : 384 + at + 128]
            v = qkv_s[rows, 768 + at : 768 + at + 128]
            a = a_s[rows, at : at + 128]
            for h in range(2):
                work.append((rows, at, slice(at + h * HEAD, at + (h + 1) * HEAD), q * keeps[h], a * keeps[h], k, v))
    sts = [nt(k, qh) for _, _, _, qh, _, k, _ in work]
    dps = [nt(v, ah) for _, _, _, _, ah, _, v in work]
    ps = []
    for st in sts:
        e = jnp.exp(st - jnp.max(st, axis=0, keepdims=True))
        ps.append(e * (1.0 / jnp.sum(e, axis=0, keepdims=True)))
    pbs = [p.astype(BF) for p in ps]
    dss = []
    for (rows, _, hr, _, _, _, _), p, pb, dp in zip(work, ps, pbs, dps):
        attn = nn(vt_s[hr, rows], pb).astype(BF)
        att_s[hr, rows] = attn
        delta = jnp.sum(at_s[hr, rows].astype(F32) * attn.astype(F32), axis=0, keepdims=True)
        dss.append((p * (dp - delta)).astype(BF))
    for i in range(0, 12, 2):
        rows, at = work[i][:2]
        dv = nn(pbs[i], work[i][4]) + nn(pbs[i + 1], work[i + 1][4])
        dk = nn(dss[i], work[i][3]) + nn(dss[i + 1], work[i + 1][3])
        dqkv_ref[rows, 768 + at : 768 + at + 128] = dv.astype(BF)
        dqkv_ref[rows, 384 + at : 384 + at + 128] = dk.astype(BF)
    for (rows, _, hr, _, _, _, _), ds in zip(work, dss):
        dqt_s[hr, rows] = nn(kt_s[hr, rows], ds).astype(BF)
    dqkv_ref[:, 0:384] = dqt_s[...].T
    part = nt(dqkv_ref[...], w_ref[...])
    for patch in range(2):
        mine_ref[patch * 128 : (patch + 1) * 128, :] = part[patch * 256 : patch * 256 + 128]
        theirs_ref[patch * 128 : (patch + 1) * 128, :] = part[patch * 256 + 128 : patch * 256 + 256].astype(BF)

    def put(i, row, value):
        ref, row = (stay_refs[i], row) if i < 4 else (go_ref, (i - 4) * 384 + row)
        ref[row : row + value.shape[0], :] = value

    for t in range(3):
        g = nn(nt_s[...], dqkv_ref[:, t * 384 : (t + 1) * 384]).astype(BF)
        for i in range(8):
            put(i, t * 96, g[i * 96 : (i + 1) * 96])
    attp = nn(selection(384, feature_order(384, at_ref[3], at_ref[1], at_ref[2])), att_s[...]).astype(BF)
    for t in range(2):
        g = nn(attp, d_s[:, t * 384 : (t + 1) * 384]).astype(BF)
        for i in range(8):
            put(i, 288 + t * 48, g[i * 48 : (i + 1) * 48])


def input_gradient_body(part_ref, got_ref, xd_ref, blocks_ref, keep_ref, o_ref, same_ref, *block_refs):
    same_ref[...] = keep_ref[...]
    for s in range(4):
        block_refs[s][...] = blocks_ref[s * 384 : (s + 1) * 384]
    outs = []
    for patch in range(2):
        xhat, inv = normalize(xd_ref[patch * 128 : patch * 128 + 128, :].astype(F32))
        dout = xd_ref[256 + patch * 128 : 256 + patch * 128 + 128, :].astype(F32)
        at = pl.ds(patch * 128, 128)
        dn = part_ref[at, :] + got_ref[at, :].astype(F32)
        first = jnp.mean(dn, axis=1, keepdims=True)
        second = jnp.mean(dn * xhat, axis=1, keepdims=True)
        outs.append((dout + inv * (dn - first - xhat * second)).reshape(16, 8, 768))
    o_ref[...] = jnp.concatenate(outs, axis=1).astype(BF)


def added(refs):
    total = refs[0][...].astype(F32)
    for ref in refs[1:]:
        total = total + ref[...].astype(F32)
    return total.astype(BF)


def split_body(at_ref, *refs):
    sel = selection(384, split_order())
    for k in range(2):
        total = added([refs[2 * i + (k ^ (step & 1))] for i, step in enumerate((2, 1, 3, 0))])
        out = nn(sel, total).astype(BF)
        rows = pl.ds((at_ref[0] ^ k) * 96, 96)
        for t in range(4):
            refs[8 + t][rows] = out[t * 96 : (t + 1) * 96]


def slot_body(back_ref, *refs):
    total = added(refs[:4])
    slot, half = slot_order()
    for h in range(2):
        part = nn(selection(128, jnp.where(half == h, slot, -1)), total).astype(BF)
        refs[4][:, :, h * 384 : (h + 1) * 384] = part.reshape(8, 16, 384)


def last_body(r_ref, ig_ref, gq_ref, go_ref, home_ref):
    sel = selection(256, home_order())
    back = lax.dot_general(
        sel, ig_ref[...].reshape(256, 768), (((0,), (0,)), ((), ())), preferred_element_type=F32
    )
    home_ref[...] = back.astype(BF)
    total = r_ref[0].astype(F32)
    for z in range(1, 8):
        total = total + r_ref[z].astype(F32)
    halves = total[0:8], total[8:16]
    for h, m in enumerate(halves):
        at = h * 384
        gq_ref[:, at : at + 384] = m[0:3, 0:384]
        gq_ref[:, 768 + at : 768 + at + 384] = m[0:3, 384:768]
        gq_ref[0:1, 1536 + at : 1536 + at + 384] = m[3:4, 0:384]
        gq_ref[1:2, 1536 + at : 1536 + at + 384] = m[3:4, 384:768]
        gq_ref[2:3, 1536 + at : 1536 + at + 384] = m[4:5, 0:384]
    go_ref[...] = halves[0][5:8] + halves[1][5:8]


def local(x, d, w_qkv, w_out):
    core, x0, y0 = (lax.axis_index(a) for a in ("c", ("x1", "x0"), "y"))
    role = core ^ ((x0 + y0) & 1)
    at = jnp.stack([core, x0, y0, role]).astype(jnp.int32)

    def swap(v):
        return lax.ppermute(v, "c", [(0, 1), (1, 0)])

    def spread(blocks, axes, steps, home):
        moved = []
        for s in steps:
            pairs = []
            for x in range(4):
                for y in range(4):
                    for k in range(2):
                        u, v = ((x + s) % 4, y) if axes[k] == "x" else (x, (y + s) % 4)
                        c, d = k ^ ((x + y) & 1), k if home else k ^ ((u + v) & 1)
                        pairs.append(((x * 2 + c) * 4 + y, (u * 2 + d) * 4 + v))
            each = len(blocks) // 4
            for block in blocks[s * each : s * each + each]:
                moved.append(lax.ppermute(block, ("x1", "x0", "c", "y"), pairs))
        return moved

    scr = lambda *s: pltpu.VMEM(s, BF)
    packed, = call(
        pack_body,
        [((16, 32, 768), BF)],
        [x.reshape(256, 768), d.reshape(256, 768)],
        scratch=[scr(256, 768), scr(256, 768), pltpu.SemaphoreType.DMA((2,))],
        hbm=(0, 1),
        limit=60,
    )
    own = lax.all_to_all(packed, ("x1", "x0", "zh0", "zh1"), split_axis=0, concat_axis=0, tiled=True)
    oth = swap(own)
    xd, *projected = call(
        own_body,
        [((512, 768), BF), ((256, 1152), BF), ((256, 384), BF), ((768, 256), BF), ((768, 1152), BF), ((384, 768), BF)],
        [at, own, w_qkv, w_out],
        scratch=[pltpu.SemaphoreType.DMA((4,))],
        smem=(0,),
        hbm=(2, 3),
        flops=10**9,
        nbytes=5 * 10**6,
        limit=46,
    )
    mine, theirs, *grads = call(
        main_body,
        [((256, 768), F32), ((256, 768), BF)] + [((384, 384), BF)] * 4 + [((1536, 384), BF)],
        [at, oth, xd, *projected],
        scratch=[scr(512, 1152), scr(512, 768), scr(512, 1152), scr(512, 384), scr(384, 512), scr(384, 512),
                 scr(384, 512), scr(384, 512), scr(384, 512), scr(768, 512)],
        smem=(0,),
        limit=32,
        flops=5 * 10**9,
        nbytes=10**7,
    )
    got = swap(theirs)
    ig, keep, *others = call(
        input_gradient_body,
        [((16, 16, 768), BF)] + [((384, 384), BF)] * 5,
        [mine, got, xd, swap(grads[4]), grads[0]],
        nbytes=3 * 10**6,
    )
    first = spread([b for pair in zip(grads[:4], others) for b in pair], "xy", (2, 1, 3), False) + [keep, others[0]]
    back = lax.all_to_all(ig, ("x1", "x0", "zh0", "zh1"), split_axis=0, concat_axis=0, tiled=True)
    second = call(split_body, [((192, 384), BF)] * 4, [at, *first], smem=(0,), flops=4_000_000_000)
    second = spread(second, "yx", (2, 1, 3, 0), True)
    slots, = call(slot_body, [((8, 16, 768), BF)], [back, *second], hbm=(0,))
    last = lax.all_to_all(slots, ("zl", "zh0", "zh1"), split_axis=0, concat_axis=0, tiled=True)
    grad_qkv, grad_out, ig_home = call(last_body, [((3, 2304), F32), ((3, 768), F32), ((256, 768), BF)], [last, back])
    return ig_home.reshape(8, 32, 768), grad_qkv, grad_out


def solution(mesh):
    fine = Mesh(mesh.devices.reshape(2, 2, 2, 2, 2, 2, 4), ("zh1", "zh0", "x1", "x0", "c", "zl", "y"))
    tm, space = ("zh1", "zh0", "x1", "x0", "c"), ("zl", "y")
    tokens, rows = P(tm, space, None), P(tm + space, None)
    return jax.shard_map(
        local,
        mesh=fine,
        in_specs=(tokens, tokens, P(), P()),
        out_specs=(tokens, rows, rows),
        check_vma=False,
    )
```

```python
import jax
import jax.numpy as jnp
from jax import lax
from jax.experimental import pallas as pl
from jax.experimental.pallas import tpu as pltpu
from jax.sharding import Mesh, PartitionSpec as P

HEAD = 64
BF = jnp.bfloat16
F32 = jnp.float32
VM = pl.BlockSpec(memory_space=pltpu.VMEM)
SM = pl.BlockSpec(memory_space=pltpu.SMEM)
HB = pl.BlockSpec(memory_space=pltpu.HBM)


def nn(a, b):
    return lax.dot_general(a, b, (((1,), (0,)), ((), ())), preferred_element_type=F32)


def nt(a, b):
    return lax.dot_general(a, b, (((1,), (1,)), ((), ())), preferred_element_type=F32)


def call(body, outs, ins, scratch=(), smem=(), hbm=(), hbm_outs=(), flops=0, nbytes=0, limit=8):
    space = {i: SM for i in smem} | {i: HB for i in hbm}
    return pl.pallas_call(
        body,
        out_shape=[jax.ShapeDtypeStruct(s, d) for s, d in outs],
        in_specs=[space.get(i, VM) for i in range(len(ins))],
        out_specs=[HB if i in hbm_outs else VM for i in range(len(outs))],
        scratch_shapes=list(scratch),
        compiler_params=pltpu.CompilerParams(vmem_limit_bytes=limit * 2**20),
        cost_estimate=pl.CostEstimate(flops=flops, bytes_accessed=nbytes, transcendentals=0),
    )(*ins)


def selection(rows, source):
    at = lax.broadcasted_iota(jnp.int32, (rows, source.shape[1]), 0)
    return (at == source).astype(F32).astype(BF)


def lanes(n):
    return lax.broadcasted_iota(jnp.int32, (1, n), 1)


def third(i):
    return (i * 21846) >> 16


def home_order():
    i = lanes(256)
    f, p = i >> 5, i & 31
    return ((p >> 1) << 4) + ((p & 1) << 3) + f


def feature_order(n, role, x0, y0):
    f = lanes(n)
    d = third(f)
    x, y = (d >> 4) & 3, d & 3
    c = ((d >> 3) ^ x ^ y) & 1
    x, y = (x - x0) & 3, (y - y0) & 3
    first, second = jnp.where(c == 0, x, y), jnp.where(c == 0, y, x)
    low = (d >> 6) * 6 + ((d >> 2) & 1) * 3 + (f - 3 * d)
    return (c ^ role) * (n // 2) + first * (n // 8) + second * (n // 32) + low


def split_order():
    i = lanes(384)
    m = jnp.where(i < 96, 0, jnp.where(i < 192, 1, 2))
    hh = jnp.where(i < 336, 0, 1)
    low, high = i - 96 * m, i - 288 - 48 * hh
    t1 = jnp.where(low < 24, 0, jnp.where(low < 48, 1, jnp.where(low < 72, 2, 3)))
    t2 = jnp.where(high < 12, 0, jnp.where(high < 24, 1, jnp.where(high < 36, 2, 3)))
    return jnp.where(i < 288, t1 * 72 + m * 24 + low, t2 * 84 + 72 + hh * 12 + high)


def slot_order():
    i = lanes(192)
    k = jnp.where(i < 96, 0, 1)
    i = i - 96 * k
    big = i < 72
    m = jnp.where(i < 24, 0, jnp.where(i < 48, 1, 2))
    hh = jnp.where(i < 84, 0, 1)
    rem = jnp.where(big, i - 24 * m, i - 72 - 12 * hh)
    d = third(rem)
    j = rem - 3 * d
    row = jnp.where(big, jnp.where(m < 2, j, 3 + (j >> 1)), 5 + j)
    half = jnp.where(big, jnp.where(m < 2, m, j & 1), hh)
    d = d + jnp.where(big, 0, 4 * k)
    slot = ((d & 1) << 2) + (d & 2) + (d >> 2)
    return (slot << 4) + (k << 3) + row, half


def pack_body(x_ref, d_ref, o_ref, x_s, d_s, p_s, sems):
    copies = [pltpu.make_async_copy(r, s, sems.at[i]) for i, (r, s) in enumerate(((x_ref, x_s), (d_ref, d_s)))]
    for copy in copies:
        copy.start()
    sel = selection(256, home_order())
    outs = []
    for i, s in enumerate((x_s, d_s)):
        copies[i].wait()
        p_s[i] = nn(sel, s[...]).astype(BF).reshape(16, 16, 768)
        outs.append(pltpu.make_async_copy(p_s.at[i], o_ref.at[:, i * 16 : i * 16 + 16, :], sems.at[2 + i]))
        outs[i].start()
    for copy in outs:
        copy.wait()


def rows_of(ref, first):
    start = first // 16 * 16
    block = ref[:, start : start + 16, :].astype(F32)
    return block[:, first - start : first - start + 8, :].reshape(128, 768)


def normalize(x):
    mean = jnp.mean(x, axis=1, keepdims=True)
    cen = x - mean
    inv = 1.0 / jnp.sqrt(jnp.mean(cen * cen, axis=1, keepdims=True) + 1e-05)
    return cen * inv, inv


def weight_copies(core, source, target, sems):
    copies = []
    for t in range(3):
        cols = pl.ds(pl.multiple_of(t * 768 + core * 384, 128), 384)
        copies.append(pltpu.make_async_copy(source.at[:, cols], target.at[:, t * 384 : (t + 1) * 384], sems.at[t]))
    return copies


def tokens_of(ref):
    x, d = ([rows_of(ref, first + patch * 8) for patch in range(2)] for first in (0, 16))
    return jnp.concatenate(x, axis=0), jnp.concatenate(d, axis=0).astype(BF)


def own_body(at_ref, own_ref, wqkv_ref, wout_ref, xd_ref, qkv_ref, a_ref, nt_ref, w_ref, wo_ref, sems):
    copies = weight_copies(at_ref[0], wqkv_ref, w_ref, sems)
    rows = pl.ds(pl.multiple_of(at_ref[0] * 384, 128), 384)
    copies.append(pltpu.make_async_copy(wout_ref.at[rows, :], wo_ref, sems.at[3]))
    for copy in copies:
        copy.start()
    x, d = tokens_of(own_ref)
    xd_ref[0:256, :] = x.astype(BF)
    xd_ref[256:512, :] = d
    n = normalize(x)[0].astype(BF)
    nt_ref[...] = nt(selection(768, feature_order(768, at_ref[3], at_ref[1], at_ref[2])), n).astype(BF)
    for t in range(3):
        copies[t].wait()
        qkv_ref[:, t * 384 : (t + 1) * 384] = nn(n, w_ref[:, t * 384 : (t + 1) * 384]).astype(BF)
    copies[3].wait()
    a_ref[...] = nt(d, wo_ref[...]).astype(BF)


def main_body(at_ref, oth_ref, xd_ref, qkv0_ref, a0_ref, nt0_ref, w_ref, wo_ref, mine_ref, theirs_ref, *rest):
    stay_refs, go_ref = rest[:4], rest[4]
    dqkv_ref, d_s, qkv_s, a_s, kt_s, vt_s, at_s, dqt_s, att_s, nt_s = rest[5:]
    x, d = tokens_of(oth_ref)
    n = normalize(x)[0].astype(BF)
    nt1 = nt(selection(768, feature_order(768, at_ref[3], at_ref[1], at_ref[2])), n).astype(BF)
    a1 = nt(d, wo_ref[...]).astype(BF)
    qkv1 = [nn(n, w_ref[:, t * 384 : (t + 1) * 384]).astype(BF) for t in range(3)]
    for patch in range(2):
        here = slice(patch * 128, (patch + 1) * 128)
        one, two = (slice(patch * 256 + side * 128, patch * 256 + side * 128 + 128) for side in range(2))
        qkv_s[one, :], a_s[one, :], nt_s[:, one] = qkv0_ref[here, :], a0_ref[here, :], nt0_ref[:, here]
        d_s[one, :] = xd_ref[256 + patch * 128 : 384 + patch * 128, :]
        a_s[two, :], nt_s[:, two], d_s[two, :] = a1[here], nt1[:, here], d[here]
        for t in range(3):
            qkv_s[two, t * 384 : (t + 1) * 384] = qkv1[t][here]
    kt_s[...] = (qkv_s[:, 384:768] * 0.125).T
    vt_s[...] = qkv_s[:, 768:1152].T
    at_s[...] = a_s[...].T
    lane = lax.broadcasted_iota(jnp.int32, (1, 128), 1)

    keeps = [((lane >= h * HEAD) & (lane < (h + 1) * HEAD)).astype(F32).astype(BF) for h in range(2)]
    work = []
    for pair in range(3):
        for patch in range(2):
            rows, at = slice(patch * 256, (patch + 1) * 256), pair * 128
            q = qkv_s[rows, at : at + 128] * 0.125
            k = qkv_s[rows, 384 + at : 384 + at + 128]
            v = qkv_s[rows, 768 + at : 768 + at + 128]
            a = a_s[rows, at : at + 128]
            for h in range(2):
                work.append((rows, at, slice(at + h * HEAD, at + (h + 1) * HEAD), q * keeps[h], a * keeps[h], k, v))
    sts = [nt(k, qh) for _, _, _, qh, _, k, _ in work]
    dps = [nt(v, ah) for _, _, _, _, ah, _, v in work]
    ps = []
    for st in sts:
        e = jnp.exp(st - jnp.max(st, axis=0, keepdims=True))
        ps.append(e * (1.0 / jnp.sum(e, axis=0, keepdims=True)))
    pbs = [p.astype(BF) for p in ps]
    dss = []
    for (rows, _, hr, _, _, _, _), p, pb, dp in zip(work, ps, pbs, dps):
        attn = nn(vt_s[hr, rows], pb).astype(BF)
        att_s[hr, rows] = attn
        delta = jnp.sum(at_s[hr, rows].astype(F32) * attn.astype(F32), axis=0, keepdims=True)
        dss.append((p * (dp - delta)).astype(BF))
    for i in range(0, 12, 2):
        rows, at = work[i][:2]
        dv = nn(pbs[i], work[i][4]) + nn(pbs[i + 1], work[i + 1][4])
        dk = nn(dss[i], work[i][3]) + nn(dss[i + 1], work[i + 1][3])
        dqkv_ref[rows, 768 + at : 768 + at + 128] = dv.astype(BF)
        dqkv_ref[rows, 384 + at : 384 + at + 128] = dk.astype(BF)
    for (rows, _, hr, _, _, _, _), ds in zip(work, dss):
        dqt_s[hr, rows] = nn(kt_s[hr, rows], ds).astype(BF)
    dqkv_ref[:, 0:384] = dqt_s[...].T
    part = nt(dqkv_ref[...], w_ref[...])
    for patch in range(2):
        mine_ref[patch * 128 : (patch + 1) * 128, :] = part[patch * 256 : patch * 256 + 128]
        theirs_ref[patch * 128 : (patch + 1) * 128, :] = part[patch * 256 + 128 : patch * 256 + 256].astype(BF)

    def put(i, row, value):
        ref, row = (stay_refs[i], row) if i < 4 else (go_ref, (i - 4) * 384 + row)
        ref[row : row + value.shape[0], :] = value

    for t in range(3):
        g = nn(nt_s[...], dqkv_ref[:, t * 384 : (t + 1) * 384]).astype(BF)
        for i in range(8):
            put(i, t * 96, g[i * 96 : (i + 1) * 96])
    attp = nn(selection(384, feature_order(384, at_ref[3], at_ref[1], at_ref[2])), att_s[...]).astype(BF)
    for t in range(2):
        g = nn(attp, d_s[:, t * 384 : (t + 1) * 384]).astype(BF)
        for i in range(8):
            put(i, 288 + t * 48, g[i * 48 : (i + 1) * 48])


def input_gradient_body(part_ref, got_ref, xd_ref, blocks_ref, keep_ref, o_ref, same_ref, *block_refs):
    same_ref[...] = keep_ref[...]
    for s in range(4):
        block_refs[s][...] = blocks_ref[s * 384 : (s + 1) * 384]
    outs = []
    for patch in range(2):
        xhat, inv = normalize(xd_ref[patch * 128 : patch * 128 + 128, :].astype(F32))
        dout = xd_ref[256 + patch * 128 : 256 + patch * 128 + 128, :].astype(F32)
        at = pl.ds(patch * 128, 128)
        dn = part_ref[at, :] + got_ref[at, :].astype(F32)
        first = jnp.mean(dn, axis=1, keepdims=True)
        second = jnp.mean(dn * xhat, axis=1, keepdims=True)
        outs.append((dout + inv * (dn - first - xhat * second)).reshape(16, 8, 768))
    o_ref[...] = jnp.concatenate(outs, axis=1).astype(BF)


def added(refs):
    total = refs[0][...].astype(F32)
    for ref in refs[1:]:
        total = total + ref[...].astype(F32)
    return total.astype(BF)


def split_body(at_ref, *refs):
    sel = selection(384, split_order())
    for k in range(2):
        total = added([refs[2 * i + (k ^ (step & 1))] for i, step in enumerate((2, 1, 3, 0))])
        out = nn(sel, total).astype(BF)
        rows = pl.ds((at_ref[0] ^ k) * 96, 96)
        for t in range(4):
            refs[8 + t][rows] = out[t * 96 : (t + 1) * 96]


def slot_body(back_ref, *refs):
    total = added(refs[:4])
    slot, half = slot_order()
    for h in range(2):
        part = nn(selection(128, jnp.where(half == h, slot, -1)), total).astype(BF)
        refs[4][:, :, h * 384 : (h + 1) * 384] = part.reshape(8, 16, 384)


def last_body(r_ref, ig_ref, gq_ref, go_ref, home_ref):
    sel = selection(256, home_order())
    back = lax.dot_general(
        sel, ig_ref[...].reshape(256, 768), (((0,), (0,)), ((), ())), preferred_element_type=F32
    )
    home_ref[...] = back.astype(BF)
    total = r_ref[0].astype(F32)
    for z in range(1, 8):
        total = total + r_ref[z].astype(F32)
    halves = total[0:8], total[8:16]
    for h, m in enumerate(halves):
        at = h * 384
        gq_ref[:, at : at + 384] = m[0:3, 0:384]
        gq_ref[:, 768 + at : 768 + at + 384] = m[0:3, 384:768]
        gq_ref[0:1, 1536 + at : 1536 + at + 384] = m[3:4, 0:384]
        gq_ref[1:2, 1536 + at : 1536 + at + 384] = m[3:4, 384:768]
        gq_ref[2:3, 1536 + at : 1536 + at + 384] = m[4:5, 0:384]
    go_ref[...] = halves[0][5:8] + halves[1][5:8]


def local(x, d, w_qkv, w_out):
    core, x0, y0 = (lax.axis_index(a) for a in ("c", ("x1", "x0"), "y"))
    role = core ^ ((x0 + y0) & 1)
    at = jnp.stack([core, x0, y0, role]).astype(jnp.int32)

    def swap(v):
        return lax.ppermute(v, "c", [(0, 1), (1, 0)])

    def spread(blocks, axes, steps):
        moved = []
        for s in steps:
            pairs = []
            for x in range(4):
                for y in range(4):
                    for k in range(2):
                        u, v = ((x + s) % 4, y) if axes[k] == "x" else (x, (y + s) % 4)
                        c, d = k ^ ((x + y) & 1), k ^ ((u + v) & 1)
                        pairs.append(((x * 2 + c) * 4 + y, (u * 2 + d) * 4 + v))
            each = len(blocks) // 4
            for block in blocks[s * each : s * each + each]:
                moved.append(lax.ppermute(block, ("x1", "x0", "c", "y"), pairs))
        return moved

    scr = lambda *s: pltpu.VMEM(s, BF)
    packed, = call(
        pack_body,
        [((16, 32, 768), BF)],
        [x.reshape(256, 768), d.reshape(256, 768)],
        scratch=[scr(256, 768), scr(256, 768), scr(2, 16, 16, 768), pltpu.SemaphoreType.DMA((4,))],
        hbm=(0, 1),
        hbm_outs=(0,),
        limit=60,
    )
    own = lax.all_to_all(packed, ("x1", "x0", "zh0", "zh1"), split_axis=0, concat_axis=0, tiled=True)
    oth = swap(own)
    xd, *projected = call(
        own_body,
        [((512, 768), BF), ((256, 1152), BF), ((256, 384), BF), ((768, 256), BF), ((768, 1152), BF), ((384, 768), BF)],
        [at, own, w_qkv, w_out],
        scratch=[pltpu.SemaphoreType.DMA((4,))],
        smem=(0,),
        hbm=(2, 3),
        flops=10**9,
        nbytes=5 * 10**6,
        limit=46,
    )
    mine, theirs, *grads = call(
        main_body,
        [((256, 768), F32), ((256, 768), BF)] + [((384, 384), BF)] * 4 + [((1536, 384), BF)],
        [at, oth, xd, *projected],
        scratch=[scr(512, 1152), scr(512, 768), scr(512, 1152), scr(512, 384), scr(384, 512), scr(384, 512),
                 scr(384, 512), scr(384, 512), scr(384, 512), scr(768, 512)],
        smem=(0,),
        limit=32,
        flops=5 * 10**9,
        nbytes=10**7,
    )
    got = swap(theirs)
    ig, keep, *others = call(
        input_gradient_body,
        [((16, 16, 768), BF)] + [((384, 384), BF)] * 5,
        [mine, got, xd, swap(grads[4]), grads[0]],
        nbytes=3 * 10**6,
    )
    first = spread([b for pair in zip(grads[:4], others) for b in pair], "xy", (2, 1, 3)) + [keep, others[0]]
    back = lax.all_to_all(ig, ("x1", "x0", "zh0", "zh1"), split_axis=0, concat_axis=0, tiled=True)
    second = call(split_body, [((192, 384), BF)] * 4, [at, *first], smem=(0,), flops=4_000_000_000)
    second = spread(second, "yx", (2, 1, 3)) + [second[0]]
    slots, = call(slot_body, [((8, 16, 768), BF)], [back, *second], hbm=(0,))
    last = lax.all_to_all(slots, ("zl", "zh0", "zh1"), split_axis=0, concat_axis=0, tiled=True)
    grad_qkv, grad_out, ig_home = call(last_body, [((3, 2304), F32), ((3, 768), F32), ((256, 768), BF)], [last, back])
    return ig_home.reshape(8, 32, 768), grad_qkv, grad_out


def solution(mesh):
    fine = Mesh(mesh.devices.reshape(2, 2, 2, 2, 2, 2, 4), ("zh1", "zh0", "x1", "x0", "c", "zl", "y"))
    tm, space = ("zh1", "zh0", "x1", "x0", "c"), ("zl", "y")
    tokens, rows = P(tm, space, None), P(tm + space, None)
    return jax.shard_map(
        local,
        mesh=fine,
        in_specs=(tokens, tokens, P(), P()),
        out_specs=(tokens, rows, rows),
        check_vma=False,
    )
```

```python
import jax
import jax.numpy as jnp
from jax import lax
from jax.experimental import pallas as pl
from jax.experimental.pallas import tpu as pltpu
from jax.sharding import Mesh, PartitionSpec as P

HEAD = 64
BF = jnp.bfloat16
F32 = jnp.float32
VM = pl.BlockSpec(memory_space=pltpu.VMEM)
SM = pl.BlockSpec(memory_space=pltpu.SMEM)
HB = pl.BlockSpec(memory_space=pltpu.HBM)


def nn(a, b):
    return lax.dot_general(a, b, (((1,), (0,)), ((), ())), preferred_element_type=F32)


def nt(a, b):
    return lax.dot_general(a, b, (((1,), (1,)), ((), ())), preferred_element_type=F32)


def call(body, outs, ins, scratch=(), smem=(), hbm=(), hbm_outs=(), flops=0, nbytes=0, limit=8):
    space = {i: SM for i in smem} | {i: HB for i in hbm}
    return pl.pallas_call(
        body,
        out_shape=[jax.ShapeDtypeStruct(s, d) for s, d in outs],
        in_specs=[space.get(i, VM) for i in range(len(ins))],
        out_specs=[HB if i in hbm_outs else VM for i in range(len(outs))],
        scratch_shapes=list(scratch),
        compiler_params=pltpu.CompilerParams(vmem_limit_bytes=limit * 2**20),
        cost_estimate=pl.CostEstimate(flops=flops, bytes_accessed=nbytes, transcendentals=0),
    )(*ins)


def selection(rows, source):
    at = lax.broadcasted_iota(jnp.int32, (rows, source.shape[1]), 0)
    return (at == source).astype(F32).astype(BF)


def lanes(n):
    return lax.broadcasted_iota(jnp.int32, (1, n), 1)


def third(i):
    return (i * 21846) >> 16


def home_order():
    i = lanes(256)
    f, p = i >> 5, i & 31
    return ((p >> 1) << 4) + ((p & 1) << 3) + f


def feature_order(n, role, x0, y0):
    f = lanes(n)
    d = third(f)
    x, y = (d >> 4) & 3, d & 3
    c = ((d >> 3) ^ x ^ y) & 1
    x, y = (x - x0) & 3, (y - y0) & 3
    first, second = jnp.where(c == 0, x, y), jnp.where(c == 0, y, x)
    low = (d >> 6) * 6 + ((d >> 2) & 1) * 3 + (f - 3 * d)
    return (c ^ role) * (n // 2) + first * (n // 8) + second * (n // 32) + low


def split_order():
    i = lanes(384)
    m = jnp.where(i < 96, 0, jnp.where(i < 192, 1, 2))
    hh = jnp.where(i < 336, 0, 1)
    low, high = i - 96 * m, i - 288 - 48 * hh
    t1 = jnp.where(low < 24, 0, jnp.where(low < 48, 1, jnp.where(low < 72, 2, 3)))
    t2 = jnp.where(high < 12, 0, jnp.where(high < 24, 1, jnp.where(high < 36, 2, 3)))
    return jnp.where(i < 288, t1 * 72 + m * 24 + low, t2 * 84 + 72 + hh * 12 + high)


def slot_order():
    i = lanes(192)
    k = jnp.where(i < 96, 0, 1)
    i = i - 96 * k
    big = i < 72
    m = jnp.where(i < 24, 0, jnp.where(i < 48, 1, 2))
    hh = jnp.where(i < 84, 0, 1)
    rem = jnp.where(big, i - 24 * m, i - 72 - 12 * hh)
    d = third(rem)
    j = rem - 3 * d
    row = jnp.where(big, jnp.where(m < 2, j, 3 + (j >> 1)), 5 + j)
    half = jnp.where(big, jnp.where(m < 2, m, j & 1), hh)
    d = d + jnp.where(big, 0, 4 * k)
    slot = ((d & 1) << 2) + (d & 2) + (d >> 2)
    return (slot << 4) + (k << 3) + row, half


def pack_body(x_ref, d_ref, o_ref, x_s, d_s, p_s, sems):
    copies = [pltpu.make_async_copy(r, s, sems.at[i]) for i, (r, s) in enumerate(((x_ref, x_s), (d_ref, d_s)))]
    for copy in copies:
        copy.start()
    sel = selection(256, home_order())
    outs = []
    for i, s in enumerate((x_s, d_s)):
        copies[i].wait()
        p_s[i] = nn(sel, s[...]).astype(BF).reshape(16, 16, 768)
        outs.append(pltpu.make_async_copy(p_s.at[i], o_ref.at[:, i * 16 : i * 16 + 16, :], sems.at[2 + i]))
        outs[i].start()
    for copy in outs:
        copy.wait()


def rows_of(ref, first):
    start = first // 16 * 16
    block = ref[:, start : start + 16, :].astype(F32)
    return block[:, first - start : first - start + 8, :].reshape(128, 768)


def normalize(x):
    mean = jnp.mean(x, axis=1, keepdims=True)
    cen = x - mean
    inv = 1.0 / jnp.sqrt(jnp.mean(cen * cen, axis=1, keepdims=True) + 1e-05)
    return cen * inv, inv


def weight_copies(core, source, target, sems):
    copies = []
    for t in range(3):
        cols = pl.ds(pl.multiple_of(t * 768 + core * 384, 128), 384)
        copies.append(pltpu.make_async_copy(source.at[:, cols], target.at[:, t * 384 : (t + 1) * 384], sems.at[t]))
    return copies


def tokens_of(ref):
    x, d = ([rows_of(ref, first + patch * 8) for patch in range(2)] for first in (0, 16))
    return jnp.concatenate(x, axis=0), jnp.concatenate(d, axis=0).astype(BF)


def own_body(at_ref, own_ref, wqkv_ref, wout_ref, xd_ref, qkv_ref, a_ref, nt_ref, w_ref, wo_ref, sems):
    copies = weight_copies(at_ref[0], wqkv_ref, w_ref, sems)
    rows = pl.ds(pl.multiple_of(at_ref[0] * 384, 128), 384)
    copies.append(pltpu.make_async_copy(wout_ref.at[rows, :], wo_ref, sems.at[3]))
    for copy in copies:
        copy.start()
    x, d = tokens_of(own_ref)
    xd_ref[0:256, :] = x.astype(BF)
    xd_ref[256:512, :] = d
    n = normalize(x)[0].astype(BF)
    nt_ref[...] = nt(selection(768, feature_order(768, at_ref[3], at_ref[1], at_ref[2])), n).astype(BF)
    for t in range(3):
        copies[t].wait()
        qkv_ref[:, t * 384 : (t + 1) * 384] = nn(n, w_ref[:, t * 384 : (t + 1) * 384]).astype(BF)
    copies[3].wait()
    a_ref[...] = nt(d, wo_ref[...]).astype(BF)


def main_body(at_ref, oth_ref, xd_ref, qkv0_ref, a0_ref, nt0_ref, w_ref, wo_ref, mine_ref, theirs_ref, *rest):
    stay_refs, go_ref = rest[:4], rest[4]
    dqkv_ref, d_s, qkv_s, a_s, kt_s, vt_s, at_s, dqt_s, att_s, nt_s = rest[5:]
    x, d = tokens_of(oth_ref)
    n = normalize(x)[0].astype(BF)
    nt1 = nt(selection(768, feature_order(768, at_ref[3], at_ref[1], at_ref[2])), n).astype(BF)
    a1 = nt(d, wo_ref[...]).astype(BF)
    qkv1 = [nn(n, w_ref[:, t * 384 : (t + 1) * 384]).astype(BF) for t in range(3)]
    for patch in range(2):
        here = slice(patch * 128, (patch + 1) * 128)
        one, two = (slice(patch * 256 + side * 128, patch * 256 + side * 128 + 128) for side in range(2))
        qkv_s[one, :], a_s[one, :], nt_s[:, one] = qkv0_ref[here, :], a0_ref[here, :], nt0_ref[:, here]
        d_s[one, :] = xd_ref[256 + patch * 128 : 384 + patch * 128, :]
        a_s[two, :], nt_s[:, two], d_s[two, :] = a1[here], nt1[:, here], d[here]
        for t in range(3):
            qkv_s[two, t * 384 : (t + 1) * 384] = qkv1[t][here]
    kt_s[...] = (qkv_s[:, 384:768] * 0.125).T
    vt_s[...] = qkv_s[:, 768:1152].T
    at_s[...] = a_s[...].T
    lane = lax.broadcasted_iota(jnp.int32, (1, 128), 1)

    keeps = [((lane >= h * HEAD) & (lane < (h + 1) * HEAD)).astype(F32).astype(BF) for h in range(2)]
    work = []
    for pair in range(3):
        for patch in range(2):
            rows, at = slice(patch * 256, (patch + 1) * 256), pair * 128
            q = qkv_s[rows, at : at + 128] * 0.125
            k = qkv_s[rows, 384 + at : 384 + at + 128]
            v = qkv_s[rows, 768 + at : 768 + at + 128]
            a = a_s[rows, at : at + 128]
            for h in range(2):
                work.append((rows, at, slice(at + h * HEAD, at + (h + 1) * HEAD), q * keeps[h], a * keeps[h], k, v))
    sts = [nt(k, qh) for _, _, _, qh, _, k, _ in work]
    dps = [nt(v, ah) for _, _, _, _, ah, _, v in work]
    ps = []
    for st in sts:
        e = jnp.exp(st - jnp.max(st, axis=0, keepdims=True))
        ps.append(e * (1.0 / jnp.sum(e, axis=0, keepdims=True)))
    pbs = [p.astype(BF) for p in ps]
    dss = []
    for (rows, _, hr, _, _, _, _), p, pb, dp in zip(work, ps, pbs, dps):
        attn = nn(vt_s[hr, rows], pb).astype(BF)
        att_s[hr, rows] = attn
        delta = jnp.sum(at_s[hr, rows].astype(F32) * attn.astype(F32), axis=0, keepdims=True)
        dss.append((p * (dp - delta)).astype(BF))
    for i in range(0, 12, 2):
        rows, at = work[i][:2]
        dv = nn(pbs[i], work[i][4]) + nn(pbs[i + 1], work[i + 1][4])
        dk = nn(dss[i], work[i][3]) + nn(dss[i + 1], work[i + 1][3])
        dqkv_ref[rows, 768 + at : 768 + at + 128] = dv.astype(BF)
        dqkv_ref[rows, 384 + at : 384 + at + 128] = dk.astype(BF)
    for (rows, _, hr, _, _, _, _), ds in zip(work, dss):
        dqt_s[hr, rows] = nn(kt_s[hr, rows], ds).astype(BF)
    dqkv_ref[:, 0:384] = dqt_s[...].T
    part = nt(dqkv_ref[...], w_ref[...])
    for patch in range(2):
        mine_ref[patch * 128 : (patch + 1) * 128, :] = part[patch * 256 : patch * 256 + 128]
        theirs_ref[patch * 128 : (patch + 1) * 128, :] = part[patch * 256 + 128 : patch * 256 + 256].astype(BF)

    def put(i, row, value):
        ref, row = (stay_refs[i], row) if i < 4 else (go_ref, (i - 4) * 384 + row)
        ref[row : row + value.shape[0], :] = value

    for t in range(3):
        g = nn(nt_s[...], dqkv_ref[:, t * 384 : (t + 1) * 384]).astype(BF)
        for i in range(8):
            put(i, t * 96, g[i * 96 : (i + 1) * 96])
    attp = nn(selection(384, feature_order(384, at_ref[3], at_ref[1], at_ref[2])), att_s[...]).astype(BF)
    for t in range(2):
        g = nn(attp, d_s[:, t * 384 : (t + 1) * 384]).astype(BF)
        for i in range(8):
            put(i, 288 + t * 48, g[i * 48 : (i + 1) * 48])


def input_gradient_body(part_ref, got_ref, xd_ref, blocks_ref, keep_ref, o_ref, same_ref, *block_refs):
    same_ref[...] = keep_ref[...]
    for s in range(4):
        block_refs[s][...] = blocks_ref[s * 384 : (s + 1) * 384]
    outs = []
    for patch in range(2):
        xhat, inv = normalize(xd_ref[patch * 128 : patch * 128 + 128, :].astype(F32))
        dout = xd_ref[256 + patch * 128 : 256 + patch * 128 + 128, :].astype(F32)
        at = pl.ds(patch * 128, 128)
        dn = part_ref[at, :] + got_ref[at, :].astype(F32)
        first = jnp.mean(dn, axis=1, keepdims=True)
        second = jnp.mean(dn * xhat, axis=1, keepdims=True)
        outs.append((dout + inv * (dn - first - xhat * second)).reshape(16, 8, 768))
    o_ref[...] = jnp.concatenate(outs, axis=1).astype(BF)


def added(refs):
    total = refs[0][...].astype(F32)
    for ref in refs[1:]:
        total = total + ref[...].astype(F32)
    return total.astype(BF)


def split_body(at_ref, *refs):
    sel = selection(384, split_order())
    for k in range(2):
        total = added([refs[2 * i + (k ^ (step & 1))] for i, step in enumerate((2, 1, 3, 0))])
        out = nn(sel, total).astype(BF)
        rows = pl.ds((at_ref[0] ^ k) * 96, 96)
        for t in range(4):
            refs[8 + t][rows] = out[t * 96 : (t + 1) * 96]


def slot_body(back_ref, *refs):
    total = added(refs[:4])
    slot, half = slot_order()
    for h in range(2):
        part = nn(selection(128, jnp.where(half == h, slot, -1)), total).astype(BF)
        refs[4][:, :, h * 384 : (h + 1) * 384] = part.reshape(8, 16, 384)


def last_body(r_ref, ig_ref, gq_ref, go_ref, home_ref, home_s, sem):
    sel = selection(256, home_order())
    back = lax.dot_general(
        sel, ig_ref[...].reshape(256, 768), (((0,), (0,)), ((), ())), preferred_element_type=F32
    )
    home_s[...] = back.astype(BF)
    copy = pltpu.make_async_copy(home_s, home_ref, sem.at[0])
    copy.start()
    total = r_ref[0].astype(F32)
    for z in range(1, 8):
        total = total + r_ref[z].astype(F32)
    halves = total[0:8], total[8:16]
    for h, m in enumerate(halves):
        at = h * 384
        gq_ref[:, at : at + 384] = m[0:3, 0:384]
        gq_ref[:, 768 + at : 768 + at + 384] = m[0:3, 384:768]
        gq_ref[0:1, 1536 + at : 1536 + at + 384] = m[3:4, 0:384]
        gq_ref[1:2, 1536 + at : 1536 + at + 384] = m[3:4, 384:768]
        gq_ref[2:3, 1536 + at : 1536 + at + 384] = m[4:5, 0:384]
    go_ref[...] = halves[0][5:8] + halves[1][5:8]
    copy.wait()


def local(x, d, w_qkv, w_out):
    core, x0, y0 = (lax.axis_index(a) for a in ("c", ("x1", "x0"), "y"))
    role = core ^ ((x0 + y0) & 1)
    at = jnp.stack([core, x0, y0, role]).astype(jnp.int32)

    def swap(v):
        return lax.ppermute(v, "c", [(0, 1), (1, 0)])

    def spread(blocks, axes, steps):
        moved = []
        for s in steps:
            pairs = []
            for x in range(4):
                for y in range(4):
                    for k in range(2):
                        u, v = ((x + s) % 4, y) if axes[k] == "x" else (x, (y + s) % 4)
                        c, d = k ^ ((x + y) & 1), k ^ ((u + v) & 1)
                        pairs.append(((x * 2 + c) * 4 + y, (u * 2 + d) * 4 + v))
            each = len(blocks) // 4
            for block in blocks[s * each : s * each + each]:
                moved.append(lax.ppermute(block, ("x1", "x0", "c", "y"), pairs))
        return moved

    scr = lambda *s: pltpu.VMEM(s, BF)
    packed, = call(
        pack_body,
        [((16, 32, 768), BF)],
        [x.reshape(256, 768), d.reshape(256, 768)],
        scratch=[scr(256, 768), scr(256, 768), scr(2, 16, 16, 768), pltpu.SemaphoreType.DMA((4,))],
        hbm=(0, 1),
        hbm_outs=(0,),
        limit=60,
    )
    own = lax.all_to_all(packed, ("x1", "x0", "zh0", "zh1"), split_axis=0, concat_axis=0, tiled=True)
    oth = swap(own)
    xd, *projected = call(
        own_body,
        [((512, 768), BF), ((256, 1152), BF), ((256, 384), BF), ((768, 256), BF), ((768, 1152), BF), ((384, 768), BF)],
        [at, own, w_qkv, w_out],
        scratch=[pltpu.SemaphoreType.DMA((4,))],
        smem=(0,),
        hbm=(2, 3),
        flops=10**9,
        nbytes=5 * 10**6,
        limit=46,
    )
    mine, theirs, *grads = call(
        main_body,
        [((256, 768), F32), ((256, 768), BF)] + [((384, 384), BF)] * 4 + [((1536, 384), BF)],
        [at, oth, xd, *projected],
        scratch=[scr(512, 1152), scr(512, 768), scr(512, 1152), scr(512, 384), scr(384, 512), scr(384, 512),
                 scr(384, 512), scr(384, 512), scr(384, 512), scr(768, 512)],
        smem=(0,),
        limit=32,
        flops=5 * 10**9,
        nbytes=10**7,
    )
    got = swap(theirs)
    ig, keep, *others = call(
        input_gradient_body,
        [((16, 16, 768), BF)] + [((384, 384), BF)] * 5,
        [mine, got, xd, swap(grads[4]), grads[0]],
        nbytes=3 * 10**6,
    )
    first = spread([b for pair in zip(grads[:4], others) for b in pair], "xy", (2, 1, 3)) + [keep, others[0]]
    back = lax.all_to_all(ig, ("x1", "x0", "zh0", "zh1"), split_axis=0, concat_axis=0, tiled=True)
    second = call(split_body, [((192, 384), BF)] * 4, [at, *first], smem=(0,), flops=4_000_000_000)
    second = spread(second, "yx", (2, 1, 3)) + [second[0]]
    slots, = call(slot_body, [((8, 16, 768), BF)], [back, *second], hbm=(0,))
    last = lax.all_to_all(slots, ("zl", "zh0", "zh1"), split_axis=0, concat_axis=0, tiled=True)
    grad_qkv, grad_out, ig_home = call(
        last_body,
        [((3, 2304), F32), ((3, 768), F32), ((256, 768), BF)],
        [last, back],
        scratch=[scr(256, 768), pltpu.SemaphoreType.DMA((1,))],
        hbm_outs=(2,),
    )
    return ig_home.reshape(8, 32, 768), grad_qkv, grad_out


def solution(mesh):
    fine = Mesh(mesh.devices.reshape(2, 2, 2, 2, 2, 2, 4), ("zh1", "zh0", "x1", "x0", "c", "zl", "y"))
    tm, space = ("zh1", "zh0", "x1", "x0", "c"), ("zl", "y")
    tokens, rows = P(tm, space, None), P(tm + space, None)
    return jax.shard_map(
        local,
        mesh=fine,
        in_specs=(tokens, tokens, P(), P()),
        out_specs=(tokens, rows, rows),
        check_vma=False,
    )
```

```python
import jax
import jax.numpy as jnp
from jax import lax
from jax.experimental import pallas as pl
from jax.experimental.pallas import tpu as pltpu
from jax.sharding import Mesh, PartitionSpec as P

HEAD = 64
BF = jnp.bfloat16
F32 = jnp.float32
VM = pl.BlockSpec(memory_space=pltpu.VMEM)
SM = pl.BlockSpec(memory_space=pltpu.SMEM)
HB = pl.BlockSpec(memory_space=pltpu.HBM)


def nn(a, b):
    return lax.dot_general(a, b, (((1,), (0,)), ((), ())), preferred_element_type=F32)


def nt(a, b):
    return lax.dot_general(a, b, (((1,), (1,)), ((), ())), preferred_element_type=F32)


def call(body, outs, ins, scratch=(), smem=(), hbm=(), hbm_outs=(), flops=0, nbytes=0, limit=8):
    space = {i: SM for i in smem} | {i: HB for i in hbm}
    return pl.pallas_call(
        body,
        out_shape=[jax.ShapeDtypeStruct(s, d) for s, d in outs],
        in_specs=[space.get(i, VM) for i in range(len(ins))],
        out_specs=[HB if i in hbm_outs else VM for i in range(len(outs))],
        scratch_shapes=list(scratch),
        compiler_params=pltpu.CompilerParams(vmem_limit_bytes=limit * 2**20),
        cost_estimate=pl.CostEstimate(flops=flops, bytes_accessed=nbytes, transcendentals=0),
    )(*ins)


def selection(rows, source):
    at = lax.broadcasted_iota(jnp.int32, (rows, source.shape[1]), 0)
    return (at == source).astype(F32).astype(BF)


def lanes(n):
    return lax.broadcasted_iota(jnp.int32, (1, n), 1)


def third(i):
    return (i * 21846) >> 16


def home_order():
    i = lanes(256)
    f, p = i >> 5, i & 31
    return ((p >> 1) << 4) + ((p & 1) << 3) + f


def feature_order(n, role, x0, y0):
    f = lanes(n)
    d = third(f)
    x, y = (d >> 4) & 3, d & 3
    c = ((d >> 3) ^ x ^ y) & 1
    x, y = (x - x0) & 3, (y - y0) & 3
    first, second = jnp.where(c == 0, x, y), jnp.where(c == 0, y, x)
    low = (d >> 6) * 6 + ((d >> 2) & 1) * 3 + (f - 3 * d)
    return (c ^ role) * (n // 2) + first * (n // 8) + second * (n // 32) + low


def split_order():
    i = lanes(384)
    m = jnp.where(i < 96, 0, jnp.where(i < 192, 1, 2))
    hh = jnp.where(i < 336, 0, 1)
    low, high = i - 96 * m, i - 288 - 48 * hh
    t1 = jnp.where(low < 24, 0, jnp.where(low < 48, 1, jnp.where(low < 72, 2, 3)))
    t2 = jnp.where(high < 12, 0, jnp.where(high < 24, 1, jnp.where(high < 36, 2, 3)))
    return jnp.where(i < 288, t1 * 72 + m * 24 + low, t2 * 84 + 72 + hh * 12 + high)


def slot_order():
    i = lanes(192)
    k = jnp.where(i < 96, 0, 1)
    i = i - 96 * k
    big = i < 72
    m = jnp.where(i < 24, 0, jnp.where(i < 48, 1, 2))
    hh = jnp.where(i < 84, 0, 1)
    rem = jnp.where(big, i - 24 * m, i - 72 - 12 * hh)
    d = third(rem)
    j = rem - 3 * d
    row = jnp.where(big, jnp.where(m < 2, j, 3 + (j >> 1)), 5 + j)
    half = jnp.where(big, jnp.where(m < 2, m, j & 1), hh)
    d = d + jnp.where(big, 0, 4 * k)
    slot = ((d & 1) << 2) + (d & 2) + (d >> 2)
    return (slot << 4) + (k << 3) + row, half


def pack_body(x_ref, d_ref, o_ref, x_s, d_s, p_s, sems):
    copies = [pltpu.make_async_copy(r, s, sems.at[i]) for i, (r, s) in enumerate(((x_ref, x_s), (d_ref, d_s)))]
    for copy in copies:
        copy.start()
    sel = selection(256, home_order())
    outs = []
    for i, s in enumerate((x_s, d_s)):
        copies[i].wait()
        p_s[i] = nn(sel, s[...]).astype(BF).reshape(16, 16, 768)
        outs.append(pltpu.make_async_copy(p_s.at[i], o_ref.at[:, i * 16 : i * 16 + 16, :], sems.at[2 + i]))
        outs[i].start()
    for copy in outs:
        copy.wait()


def rows_of(ref, first):
    start = first // 16 * 16
    block = ref[:, start : start + 16, :].astype(F32)
    return block[:, first - start : first - start + 8, :].reshape(128, 768)


def normalize(x):
    mean = jnp.mean(x, axis=1, keepdims=True)
    cen = x - mean
    inv = 1.0 / jnp.sqrt(jnp.mean(cen * cen, axis=1, keepdims=True) + 1e-05)
    return cen * inv, inv


def weight_copies(core, source, target, sems):
    copies = []
    for t in range(3):
        cols = pl.ds(pl.multiple_of(t * 768 + core * 384, 128), 384)
        copies.append(pltpu.make_async_copy(source.at[:, cols], target.at[:, t * 384 : (t + 1) * 384], sems.at[t]))
    return copies


def tokens_of(ref):
    x, d = ([rows_of(ref, first + patch * 8) for patch in range(2)] for first in (0, 16))
    return jnp.concatenate(x, axis=0), jnp.concatenate(d, axis=0).astype(BF)


def own_body(at_ref, own_ref, wqkv_ref, wout_ref, xd_ref, qkv_ref, a_ref, nt_ref, w_ref, wo_ref, sems):
    copies = weight_copies(at_ref[0], wqkv_ref, w_ref, sems)
    rows = pl.ds(pl.multiple_of(at_ref[0] * 384, 128), 384)
    copies.append(pltpu.make_async_copy(wout_ref.at[rows, :], wo_ref, sems.at[3]))
    for copy in copies:
        copy.start()
    x, d = tokens_of(own_ref)
    xd_ref[0:256, :] = x.astype(BF)
    xd_ref[256:512, :] = d
    n = normalize(x)[0].astype(BF)
    nt_ref[...] = nt(selection(768, feature_order(768, at_ref[3], at_ref[1], at_ref[2])), n).astype(BF)
    for t in range(3):
        copies[t].wait()
        qkv_ref[:, t * 384 : (t + 1) * 384] = nn(n, w_ref[:, t * 384 : (t + 1) * 384]).astype(BF)
    copies[3].wait()
    a_ref[...] = nt(d, wo_ref[...]).astype(BF)


def main_body(at_ref, oth_ref, xd_ref, qkv0_ref, a0_ref, nt0_ref, w_ref, wo_ref, mine_ref, theirs_ref, *rest):
    stay_refs, go_ref = rest[:4], rest[4]
    dqkv_ref, d_s, qkv_s, a_s, kt_s, vt_s, at_s, dqt_s, att_s, nt_s = rest[5:]
    x, d = tokens_of(oth_ref)
    n = normalize(x)[0].astype(BF)
    nt1 = nt(selection(768, feature_order(768, at_ref[3], at_ref[1], at_ref[2])), n).astype(BF)
    a1 = nt(d, wo_ref[...]).astype(BF)
    qkv1 = [nn(n, w_ref[:, t * 384 : (t + 1) * 384]).astype(BF) for t in range(3)]
    for patch in range(2):
        here = slice(patch * 128, (patch + 1) * 128)
        one, two = (slice(patch * 256 + side * 128, patch * 256 + side * 128 + 128) for side in range(2))
        qkv_s[one, :], a_s[one, :], nt_s[:, one] = qkv0_ref[here, :], a0_ref[here, :], nt0_ref[:, here]
        d_s[one, :] = xd_ref[256 + patch * 128 : 384 + patch * 128, :]
        a_s[two, :], nt_s[:, two], d_s[two, :] = a1[here], nt1[:, here], d[here]
        for t in range(3):
            qkv_s[two, t * 384 : (t + 1) * 384] = qkv1[t][here]
    kt_s[...] = (qkv_s[:, 384:768] * 0.125).T
    vt_s[...] = qkv_s[:, 768:1152].T
    at_s[...] = a_s[...].T
    lane = lax.broadcasted_iota(jnp.int32, (1, 128), 1)

    keeps = [((lane >= h * HEAD) & (lane < (h + 1) * HEAD)).astype(F32).astype(BF) for h in range(2)]
    work = []
    for pair in range(3):
        for patch in range(2):
            rows, at = slice(patch * 256, (patch + 1) * 256), pair * 128
            q = qkv_s[rows, at : at + 128] * 0.125
            k = qkv_s[rows, 384 + at : 384 + at + 128]
            v = qkv_s[rows, 768 + at : 768 + at + 128]
            a = a_s[rows, at : at + 128]
            for h in range(2):
                work.append((rows, at, slice(at + h * HEAD, at + (h + 1) * HEAD), q * keeps[h], a * keeps[h], k, v))
    sts = [nt(k, qh) for _, _, _, qh, _, k, _ in work]
    dps = [nt(v, ah) for _, _, _, _, ah, _, v in work]
    ps = []
    for st in sts:
        e = jnp.exp(st - jnp.max(st, axis=0, keepdims=True))
        ps.append(e * (1.0 / jnp.sum(e, axis=0, keepdims=True)))
    pbs = [p.astype(BF) for p in ps]
    dss = []
    for (rows, _, hr, _, _, _, _), p, pb, dp in zip(work, ps, pbs, dps):
        attn = nn(vt_s[hr, rows], pb).astype(BF)
        att_s[hr, rows] = attn
        delta = jnp.sum(at_s[hr, rows].astype(F32) * attn.astype(F32), axis=0, keepdims=True)
        dss.append((p * (dp - delta)).astype(BF))
    for i in range(0, 12, 2):
        rows, at = work[i][:2]
        dv = nn(pbs[i], work[i][4]) + nn(pbs[i + 1], work[i + 1][4])
        dk = nn(dss[i], work[i][3]) + nn(dss[i + 1], work[i + 1][3])
        dqkv_ref[rows, 768 + at : 768 + at + 128] = dv.astype(BF)
        dqkv_ref[rows, 384 + at : 384 + at + 128] = dk.astype(BF)
    for (rows, _, hr, _, _, _, _), ds in zip(work, dss):
        dqt_s[hr, rows] = nn(kt_s[hr, rows], ds).astype(BF)
    dqkv_ref[:, 0:384] = dqt_s[...].T
    part = nt(dqkv_ref[...], w_ref[...])
    for patch in range(2):
        mine_ref[patch * 128 : (patch + 1) * 128, :] = part[patch * 256 : patch * 256 + 128]
        theirs_ref[patch * 128 : (patch + 1) * 128, :] = part[patch * 256 + 128 : patch * 256 + 256].astype(BF)

    def put(i, row, value):
        ref, row = (stay_refs[i], row) if i < 4 else (go_ref, (i - 4) * 384 + row)
        ref[row : row + value.shape[0], :] = value

    for t in range(3):
        g = nn(nt_s[...], dqkv_ref[:, t * 384 : (t + 1) * 384]).astype(BF)
        for i in range(8):
            put(i, t * 96, g[i * 96 : (i + 1) * 96])
    attp = nn(selection(384, feature_order(384, at_ref[3], at_ref[1], at_ref[2])), att_s[...]).astype(BF)
    for t in range(2):
        g = nn(attp, d_s[:, t * 384 : (t + 1) * 384]).astype(BF)
        for i in range(8):
            put(i, 288 + t * 48, g[i * 48 : (i + 1) * 48])


def input_gradient_body(part_ref, got_ref, xd_ref, blocks_ref, keep_ref, o_ref, same_ref, *block_refs):
    same_ref[...] = keep_ref[...]
    for s in range(4):
        block_refs[s][...] = blocks_ref[s * 384 : (s + 1) * 384]
    outs = []
    for patch in range(2):
        xhat, inv = normalize(xd_ref[patch * 128 : patch * 128 + 128, :].astype(F32))
        dout = xd_ref[256 + patch * 128 : 256 + patch * 128 + 128, :].astype(F32)
        at = pl.ds(patch * 128, 128)
        dn = part_ref[at, :] + got_ref[at, :].astype(F32)
        first = jnp.mean(dn, axis=1, keepdims=True)
        second = jnp.mean(dn * xhat, axis=1, keepdims=True)
        outs.append((dout + inv * (dn - first - xhat * second)).reshape(16, 8, 768))
    o_ref[...] = jnp.concatenate(outs, axis=1).astype(BF)


def added(refs):
    total = refs[0][...].astype(F32)
    for ref in refs[1:]:
        total = total + ref[...].astype(F32)
    return total.astype(BF)


def split_body(at_ref, *refs):
    sel = selection(384, split_order())
    for k in range(2):
        total = added([refs[2 * i + (k ^ (step & 1))] for i, step in enumerate((2, 1, 3, 0))])
        out = nn(sel, total).astype(BF)
        rows = pl.ds((at_ref[0] ^ k) * 96, 96)
        for t in range(4):
            refs[8 + t][rows] = out[t * 96 : (t + 1) * 96]


def slot_body(back_ref, *refs):
    total = added(refs[:4])
    slot, half = slot_order()
    for h in range(2):
        part = nn(selection(128, jnp.where(half == h, slot, -1)), total).astype(BF)
        refs[4][:, :, h * 384 : (h + 1) * 384] = part.reshape(8, 16, 384)


def last_body(r_ref, ig_ref, gq_ref, go_ref, home_ref):
    sel = selection(256, home_order())
    back = lax.dot_general(
        sel, ig_ref[...].reshape(256, 768), (((0,), (0,)), ((), ())), preferred_element_type=F32
    )
    home_ref[...] = back.astype(BF)
    total = r_ref[0].astype(F32)
    for z in range(1, 8):
        total = total + r_ref[z].astype(F32)
    halves = total[0:8], total[8:16]
    for h, m in enumerate(halves):
        at = h * 384
        gq_ref[:, at : at + 384] = m[0:3, 0:384]
        gq_ref[:, 768 + at : 768 + at + 384] = m[0:3, 384:768]
        gq_ref[0:1, 1536 + at : 1536 + at + 384] = m[3:4, 0:384]
        gq_ref[1:2, 1536 + at : 1536 + at + 384] = m[3:4, 384:768]
        gq_ref[2:3, 1536 + at : 1536 + at + 384] = m[4:5, 0:384]
    go_ref[...] = halves[0][5:8] + halves[1][5:8]


def local(x, d, w_qkv, w_out):
    core, x0, y0 = (lax.axis_index(a) for a in ("c", ("x1", "x0"), "y"))
    role = core ^ ((x0 + y0) & 1)
    at = jnp.stack([core, x0, y0, role]).astype(jnp.int32)

    def swap(v):
        return lax.ppermute(v, "c", [(0, 1), (1, 0)])

    def spread(blocks, axes, steps):
        moved = []
        for s in steps:
            pairs = []
            for x in range(4):
                for y in range(4):
                    for k in range(2):
                        u, v = ((x + s) % 4, y) if axes[k] == "x" else (x, (y + s) % 4)
                        c, d = k ^ ((x + y) & 1), k ^ ((u + v) & 1)
                        pairs.append(((x * 2 + c) * 4 + y, (u * 2 + d) * 4 + v))
            each = len(blocks) // 4
            for block in blocks[s * each : s * each + each]:
                moved.append(lax.ppermute(block, ("x1", "x0", "c", "y"), pairs))
        return moved

    scr = lambda *s: pltpu.VMEM(s, BF)
    packed, = call(
        pack_body,
        [((16, 32, 768), BF)],
        [x.reshape(256, 768), d.reshape(256, 768)],
        scratch=[scr(256, 768), scr(256, 768), scr(2, 16, 16, 768), pltpu.SemaphoreType.DMA((4,))],
        hbm=(0, 1),
        hbm_outs=(0,),
        limit=60,
    )
    own = lax.all_to_all(packed, ("x1", "x0", "zh0", "zh1"), split_axis=0, concat_axis=0, tiled=True)
    oth = swap(own)
    xd, *projected = call(
        own_body,
        [((512, 768), BF), ((256, 1152), BF), ((256, 384), BF), ((768, 256), BF), ((768, 1152), BF), ((384, 768), BF)],
        [at, own, w_qkv, w_out],
        scratch=[pltpu.SemaphoreType.DMA((4,))],
        smem=(0,),
        hbm=(2, 3),
        flops=10**9,
        nbytes=5 * 10**6,
        limit=46,
    )
    mine, theirs, *grads = call(
        main_body,
        [((256, 768), F32), ((256, 768), BF)] + [((384, 384), BF)] * 4 + [((1536, 384), BF)],
        [at, oth, xd, *projected],
        scratch=[scr(512, 1152), scr(512, 768), scr(512, 1152), scr(512, 384), scr(384, 512), scr(384, 512),
                 scr(384, 512), scr(384, 512), scr(384, 512), scr(768, 512)],
        smem=(0,),
        limit=24,
        flops=5 * 10**9,
        nbytes=10**7,
    )
    got = swap(theirs)
    ig, keep, *others = call(
        input_gradient_body,
        [((16, 16, 768), BF)] + [((384, 384), BF)] * 5,
        [mine, got, xd, swap(grads[4]), grads[0]],
        nbytes=3 * 10**6,
    )
    first = spread([b for pair in zip(grads[:4], others) for b in pair], "xy", (2, 1, 3)) + [keep, others[0]]
    back = lax.all_to_all(ig, ("x1", "x0", "zh0", "zh1"), split_axis=0, concat_axis=0, tiled=True)
    second = call(split_body, [((192, 384), BF)] * 4, [at, *first], smem=(0,), flops=4_000_000_000)
    second = spread(second, "yx", (2, 1, 3)) + [second[0]]
    slots, = call(slot_body, [((8, 16, 768), BF)], [back, *second], hbm=(0,))
    last = lax.all_to_all(slots, ("zl", "zh0", "zh1"), split_axis=0, concat_axis=0, tiled=True)
    grad_qkv, grad_out, ig_home = call(last_body, [((3, 2304), F32), ((3, 768), F32), ((256, 768), BF)], [last, back])
    return ig_home.reshape(8, 32, 768), grad_qkv, grad_out


def solution(mesh):
    fine = Mesh(mesh.devices.reshape(2, 2, 2, 2, 2, 2, 4), ("zh1", "zh0", "x1", "x0", "c", "zl", "y"))
    tm, space = ("zh1", "zh0", "x1", "x0", "c"), ("zl", "y")
    tokens, rows = P(tm, space, None), P(tm + space, None)
    return jax.shard_map(
        local,
        mesh=fine,
        in_specs=(tokens, tokens, P(), P()),
        out_specs=(tokens, rows, rows),
        check_vma=False,
    )
```
